32 devices in a mesh: expert: 8 (over y, x, core), shard: 4 (over z).
Axes of the slice: x: 2, y: 2, z: 4, core: 2. Of those that a mesh axis runs over, the one named last changes fastest.
Arguments:
- head_outputs: bfloat16 [4096, 1024], P(('expert', 'shard')), may hold values from -6 to 6
- residual: bfloat16 [4096, 1024], P(('expert', 'shard')), may hold values from -4 to 4
- output_weight: bfloat16 [1024, 1024], P('shard'), may hold values from -0.1875 to 0.1875
- router: bfloat16 [1024, 32], replicated, may hold values from -0.095703125 to 0.095703125
- norm_gain: float32 [1024], replicated, may hold values from 0.1 to 1.9
- placed_gate_up: bfloat16 [64, 1024, 1024], P('expert', 'shard'), may hold values from -0.1875 to 0.1875
- placed_down: bfloat16 [64, 512, 1024], P('expert', 'shard'), may hold values from -0.25 to 0.25
- routes: int32 [4096, 8], P(('expert', 'shard')), may hold values from 0 to 31, all different within a row; in each aligned block of 128 rows (0 to 127, 128 to 255, ...) at most 48 rows name the same one
- replica_pick: int32 [4096, 8], P(('expert', 'shard')), may hold values from 0 to 5
- placement: int32 [64], replicated, may hold values from 0 to 31, as said below
- final_gain: float32 [1024], replicated, may hold values from 0.1 to 1.9
Outputs:
- next_input: bfloat16 [4096, 1024], P(('expert', 'shard'))
The draws below stay inside these ranges and needn't reach their ends.
Inputs may be any that keep to these rules, and one draw needn't show every extreme that they name: `routes`: each token names 8 different experts. Among the 128 tokens of one device no expert is named more than 48 times, and in some device's tokens one expert is named exactly 48 times. `placement`: every expert holds one to three of the 64 placements: a quarter of the experts hold three, half of them two, the rest one.
All inputs are finite; a program needn't handle non-finite values.
Results may differ from the reference program's by a relative error of at most 0.011.
Values may be sent and summed in bfloat16 or wider, within the bound.
No kernel may reach another device: no remote copies, remote signals or barrier semaphores. Data moves between devices by JAX's collectives and lax.ppermute only.
A program may use at most 128 MiB of HBM per device.

```python
import math
import jax
import jax.numpy as jnp
import numpy as np
from jax import lax

D = 1024
FF = 512
EXPERTS = 32
TOP = 8
TOK_DEV = 128
CAP = 48
PL = 64
TOKENS = 4096


def draw_placement(key, part):
    shuffled = jax.random.permutation(jax.random.fold_in(key, 11), EXPERTS).astype(jnp.int32)
    quarter = EXPERTS // 4
    half_count = EXPERTS // 2
    copies = np.array([3] * quarter + [2] * half_count + [1] * (EXPERTS - quarter - half_count))
    listed = jnp.repeat(shuffled, copies, total_repeat_length=PL)
    return jax.random.permutation(jax.random.fold_in(key, 12), listed).astype(jnp.int32)


def plant(values, rng, least, high):
    extent = values.shape
    index_at = [jax.random.randint(jax.random.fold_in(rng, axis), (), 0, extent[axis]) for axis in range(len(extent))]
    values = values.at[tuple(index_at)].set(least)
    longest = extent.index(max(extent))
    index_at[longest] = (index_at[longest] + 1) % extent[longest]
    return values.at[tuple(index_at)].set(high)


def block_scale(stream_key, dims, split, least, high):
    def one(dim, parts):
        heights = jax.random.uniform(jax.random.fold_in(jax.random.fold_in(stream_key, 6), dim), (parts,), jnp.float32, least / len(split), high / len(split))
        return jnp.repeat(jnp.exp(heights), dims[dim] // parts).reshape((-1,) + (1,) * (len(dims) - dim - 1))

    gain = one(*split[0])
    for cut in split[1:]:
        gain = gain * one(*cut)
    return gain


def deal_out(key, own, number, rows, amount, top, reach, skew):
    order = jax.random.permutation(key, amount)
    packed, usual = portions_of(amount, rows * top, reach, skew, True), portions_of(amount, rows * top, reach, skew, False)
    places = jnp.arange(amount)

    def named(sizes, rotation):
        used = int((sizes > 0).sum())
        fixed = max(1, used // 4)
        moved = fixed + (places - fixed + rotation * (used - fixed)) % max(1, amount - fixed)
        return jnp.zeros((amount,), jnp.int32).at[order[jnp.where(places < fixed, places, moved)]].set(jnp.asarray(sizes, jnp.int32))

    sizes = jnp.where(number % 4 == 0, named(packed, number // 4), named(usual, number - number // 4 - 1))
    mixed = jax.random.permutation(jax.random.fold_in(own, 3), amount)
    giver, sink = mixed[0:amount // 2 * 2:2], mixed[1:amount // 2 * 2:2]
    room = jnp.minimum(sizes[giver] - 1, reach - sizes[sink]) // 2
    room = jnp.where((giver == order[0]) | (sink == order[0]) | (sizes[sink] == 0), 0, jnp.maximum(room, 0))
    moved = jax.random.randint(jax.random.fold_in(own, 4), (amount // 2,), 0, 1 << 20) % (room + 1)
    sizes = sizes.at[giver].add(-moved).at[sink].add(moved)
    items = jnp.searchsorted(jnp.cumsum(sizes), jnp.arange(rows * top), side="right").astype(jnp.int32)
    table = items.reshape(top, rows).T
    table = table[jax.random.permutation(jax.random.fold_in(own, 1), rows)]
    rotation = jax.random.randint(jax.random.fold_in(own, 2), (rows, 1), 0, top)
    return jnp.take_along_axis(table, (jnp.arange(top)[None, :] + rotation) % top, axis=1)


def portions_of(number_of, total, bound, lean, full):
    loads = [(1 << 20) // math.isqrt(standing ** lean) + 1 for standing in range(1, number_of + 1)]
    largest = bound if full else min(bound, max(-(-total // number_of), total * loads[0] // sum(loads)))
    least = 1 if total - largest >= number_of - 1 else 0
    given, spare = [largest] + [least] * (number_of - 1), total - largest - least * (number_of - 1)
    while spare > 0:
        candidates = [i for i in range(1, number_of) if given[i] < largest] or [i for i in range(1, number_of) if given[i] < bound]
        mass, remaining = sum([loads[i] for i in candidates]), spare
        for i in candidates:
            extra = min(bound - given[i], max(1, remaining * loads[i] // mass), spare)
            given[i] = given[i] + extra
            spare = spare - extra
    return np.array(given)


def bell_draw(stream_key, shape, width, most, shards=(), kind=jnp.bfloat16):
    values = width * jax.random.normal(stream_key, shape, jnp.float32)
    if shards:
        values = values * block_scale(stream_key, shape, shards, -0.22, 0.18)
    return jnp.clip(values, -most, most).astype(kind)


def setup_inputs(seed: int = 0) -> dict:
    seeds = jax.random.split(jax.random.key(seed), 12)
    head_outputs = bell_draw(seeds[0], (TOKENS, D), 1.0, 6.0, ((0, 32),))
    residual = bell_draw(seeds[1], (TOKENS, D), 0.5, 4.0, ((0, 32),))
    output_weight = bell_draw(seeds[2], (D, D), D ** -0.5, 0.1875, ((0, 4),))
    router = bell_draw(seeds[3], (D, EXPERTS), 0.016, 0.095703125)
    norm_gain = jnp.clip(1.0 + 0.18 * jax.random.normal(seeds[4], (D,), jnp.float32), 0.1, 1.9)
    placed_gate_up = bell_draw(seeds[5], (PL, D, 2 * FF), D ** -0.5, 0.1875, ((0, 8), (1, 4)))
    placed_down = bell_draw(seeds[6], (PL, FF, D), FF ** -0.5, 0.25, ((0, 8), (1, 4)))
    routes_keys = jax.random.split(jax.random.fold_in(seeds[7], 1), TOKENS // TOK_DEV)
    routes_turns = jax.random.permutation(jax.random.fold_in(seeds[7], 3), TOKENS // TOK_DEV)
    routes = jax.vmap(lambda own, number: deal_out(jax.random.fold_in(seeds[7], 2), own, number, TOK_DEV, EXPERTS, TOP, CAP, 2))(routes_keys, routes_turns).reshape((TOKENS, TOP))
    replica_pick = plant(jax.random.randint(seeds[8], (TOKENS, TOP), 0, 6), jax.random.fold_in(seeds[8], 1), 0, 5).astype(jnp.int32)
    placement = draw_placement(jax.random.fold_in(seeds[11], 71), 0)
    final_gain = jnp.clip(1.0 + 0.18 * jax.random.normal(seeds[10], (D,), jnp.float32), 0.1, 1.9)
    return {"head_outputs": head_outputs, "residual": residual, "output_weight": output_weight, "router": router, "norm_gain": norm_gain, "placed_gate_up": placed_gate_up, "placed_down": placed_down, "routes": routes, "replica_pick": replica_pick, "placement": placement, "final_gain": final_gain}


eps_norm = 1e-06
most_copies = 3

def rms_scale(values, scale_gain):
    mean_square = lax.optimization_barrier(jnp.mean(values * values, axis=-1, keepdims=True))
    return values * lax.rsqrt(mean_square + eps_norm) * scale_gain

def choose_slots(routes, replica_pick, placement, experts):
    labels = jnp.arange(experts, dtype=jnp.int32)
    holder_mask = (placement[None, :] == labels[:, None]).astype(jnp.int32)
    before = (jnp.cumsum(holder_mask, axis=1) - holder_mask).astype(jnp.int32)
    copies = lax.optimization_barrier(jnp.sum(holder_mask, axis=1)).astype(jnp.int32)
    places = jnp.arange(placement.shape[0], dtype=jnp.int32)
    route_hits = (routes[..., None] == labels).astype(jnp.int32)
    held_count = lax.optimization_barrier(jnp.sum(route_hits * copies, axis=-1)).astype(jnp.int32)
    wanted = (replica_pick % held_count).astype(jnp.int32)
    chosen = jnp.zeros(routes.shape, jnp.int32)
    for replica in range(most_copies):
        column = lax.optimization_barrier(jnp.sum(holder_mask * (before == replica).astype(jnp.int32) * places[None, :], axis=1)).astype(jnp.int32)
        candidate = lax.optimization_barrier(jnp.sum(route_hits * column, axis=-1)).astype(jnp.int32)
        chosen = jnp.where(wanted == replica, candidate, chosen)
    return chosen

def expert_block(block_rows, gate_up_weight, down_weight):
    both_parts = jnp.dot(block_rows.astype(jnp.float32), gate_up_weight.astype(jnp.float32))
    hidden_units = down_weight.shape[0]
    activated = (jax.nn.silu(both_parts[:, :hidden_units]) * both_parts[:, hidden_units:]).astype(jnp.bfloat16)
    return jnp.dot(activated.astype(jnp.float32), down_weight.astype(jnp.float32)).astype(jnp.bfloat16)

def reference(head_outputs, residual, output_weight, router, norm_gain, placed_gate_up, placed_down, routes, replica_pick, placement, final_gain):
    projected = jnp.dot(head_outputs.astype(jnp.float32), output_weight.astype(jnp.float32))
    hidden = (residual.astype(jnp.float32) + projected).astype(jnp.bfloat16)
    hidden_wide = hidden.astype(jnp.float32)
    normed = rms_scale(hidden_wide, norm_gain).astype(jnp.bfloat16)
    logits = jnp.dot(normed.astype(jnp.float32), router.astype(jnp.float32))
    labels = jnp.arange(EXPERTS, dtype=jnp.int32)
    selector = (routes[..., None] == labels).astype(jnp.float32)
    chosen_logits = lax.optimization_barrier(jnp.sum(selector * logits[:, None, :], axis=-1))
    raised = jnp.exp(chosen_logits)
    route_weight = raised / lax.optimization_barrier(jnp.sum(raised, axis=-1, keepdims=True))
    slot_ids = choose_slots(routes, replica_pick, placement, EXPERTS).reshape(-1)
    count_all = TOKENS * TOP
    counts = jnp.zeros((PL,), jnp.int32).at[slot_ids].add(jnp.ones((count_all,), jnp.int32))
    sort_order = jnp.argsort(slot_ids, stable=True).astype(jnp.int32)
    sorted_slots = slot_ids[sort_order]
    firsts = (jnp.cumsum(counts) - counts).astype(jnp.int32)
    rank_sorted = (jnp.arange(count_all, dtype=jnp.int32) - firsts[sorted_slots]).astype(jnp.int32)
    slot_rank = jnp.zeros((count_all,), jnp.int32).at[sort_order].set(rank_sorted)
    block_size = 512
    padded_len = ((counts + block_size - 1) // block_size * block_size).astype(jnp.int32)
    padded_start = (jnp.cumsum(padded_len) - padded_len).astype(jnp.int32)
    position = (padded_start[slot_ids] + slot_rank).astype(jnp.int32)
    block_count = count_all // block_size + PL
    owner_table = jnp.full((block_count * block_size,), -1, jnp.int32).at[position].set(jnp.arange(count_all, dtype=jnp.int32))
    owner_table = owner_table.reshape(block_count, block_size)
    slot_ends = padded_start + padded_len
    block_starts = jnp.arange(block_count, dtype=jnp.int32) * block_size
    block_slot = jnp.minimum(lax.optimization_barrier(jnp.sum((slot_ends[None, :] <= block_starts[:, None]).astype(jnp.int32), axis=1)), PL - 1).astype(jnp.int32)
    flat_weight = route_weight.reshape(-1)

    def add_block(running_sum, item_pair):
        owner_ids, slot_here = item_pair
        is_live = owner_ids >= 0
        safe_ids = jnp.maximum(owner_ids, 0).astype(jnp.int32)
        row_ids = (safe_ids // TOP).astype(jnp.int32)
        block_out = expert_block(normed[row_ids], placed_gate_up[slot_here], placed_down[slot_here])
        weighted = jnp.where(is_live[:, None], flat_weight[safe_ids][:, None] * block_out.astype(jnp.float32), jnp.zeros((), jnp.float32))
        return (running_sum.at[row_ids].add(weighted), None)
    mixture, _ = lax.scan(add_block, jnp.zeros((TOKENS, D), jnp.float32), (owner_table, block_slot))
    return rms_scale(hidden_wide + mixture, final_gain).astype(jnp.bfloat16)
```

```python
import functools
import math

import jax
import jax.numpy as jnp
from jax import lax
from jax.experimental import pallas as pl
from jax.experimental.pallas import tpu as pltpu
from jax.sharding import PartitionSpec as P

CAP = 48


eps_norm = 1e-06
most_copies = 3


def rms_scale(values, scale_gain):
    mean_square = jnp.mean(values * values, axis=-1, keepdims=True)
    return values * lax.rsqrt(mean_square + eps_norm) * scale_gain


bf16 = jnp.bfloat16
f32 = jnp.float32
vmem_limit = 48 * 1024 * 1024
row_tile = 256
chunk_slots = 2


def swap(value, axis, bits):
    size = lax.axis_size(axis)
    return lax.ppermute(value, axis, [(i, i ^ bits) for i in range(size)])


def hit_table(routes, replica_pick, placement):
    same = placement[:, None] == placement[None, :]
    place = jnp.arange(placement.shape[0], dtype=jnp.int32)
    copies = jnp.sum(same.astype(jnp.int32), axis=1)
    rank = jnp.sum((same & (place[None, :] < place[:, None])).astype(jnp.int32), axis=1)
    named = routes[:, :, None] == placement
    picked = lax.rem(replica_pick[:, :, None], jnp.broadcast_to(copies, named.shape)) == rank
    return jnp.any(named & picked, axis=1).astype(f32)


def project_kernel(where_ref, heads_ref, residual_ref, gain_ref, router_ref, hits_ref, mine_ref, other_ref, rows_ref, hidden_ref, weight, sems):
    e = where_ref[0]
    s = where_ref[1]
    piece = mine_ref.shape[2]
    chips, shards = mine_ref.shape[0], mine_ref.shape[1]
    depth = weight.shape[0] // shards
    copies = []
    for core, source in enumerate((mine_ref, other_ref)):
        for chip in range(chips):
            for k in range(shards):
                start = pl.multiple_of((s ^ k) * depth + (e ^ (2 * chip + core)) * piece, piece)
                copies.append(
                    pltpu.make_async_copy(
                        source.at[chip, k],
                        weight.at[pl.ds(start, piece), :],
                        sems.at[(core * chips + chip) * shards + k],
                    )
                )
    for copy in copies:
        copy.start()
    for copy in copies:
        copy.wait()
    projected = jnp.dot(heads_ref[...], weight[...], preferred_element_type=f32)
    hidden = (residual_ref[...].astype(f32) + projected).astype(bf16)
    hidden_ref[...] = hidden
    normed = rms_scale(hidden.astype(f32), gain_ref[...]).astype(bf16)
    width = normed.shape[1]
    rows_ref[:, :width] = normed
    logits = jnp.dot(normed, router_ref[...], preferred_element_type=f32)
    places = logits.shape[1] // 2
    raised = jnp.where(hits_ref[...] > 0, jnp.exp(logits), 0.0)
    total = jnp.sum(raised, axis=-1, keepdims=True) * 0.5
    share = raised / total
    high = share.astype(bf16)
    low = (share - high.astype(f32)).astype(bf16)
    lane = lax.broadcasted_iota(jnp.int32, share.shape, 1)
    rows_ref[:, width:] = jnp.where(lane < places, high.astype(f32), low.astype(f32)).astype(bf16)


def project(where, heads, residual, gain, router_pairs, hits, mine, other):
    rows, width = residual.shape
    pieces = 2 * mine.shape[0] * mine.shape[1]
    vm = pl.BlockSpec(memory_space=pltpu.VMEM)
    hbm = pl.BlockSpec(memory_space=pl.ANY)
    return pl.pallas_call(
        project_kernel,
        out_shape=(
            jax.ShapeDtypeStruct((rows, width + router_pairs.shape[1]), bf16),
            jax.ShapeDtypeStruct((rows, width), bf16),
        ),
        in_specs=[pl.BlockSpec(memory_space=pltpu.SMEM), vm, vm, vm, vm, vm, hbm, hbm],
        out_specs=(vm, vm),
        scratch_shapes=[
            pltpu.VMEM((width, width), bf16),
            pltpu.SemaphoreType.DMA((pieces,)),
        ],
        compiler_params=pltpu.CompilerParams(vmem_limit_bytes=vmem_limit),
        cost_estimate=pl.CostEstimate(flops=2 * rows * width * width, bytes_accessed=3 * width * width, transcendentals=rows * 128),
        name="project",
    )(where, heads, residual, gain, router_pairs, hits, mine, other)


def load_weights(where_ref, sources, weight, sems):
    s = where_ref[1]
    depth = sources[0].shape[1]
    copies = []
    for k, source in enumerate(sources):
        start = pl.multiple_of((s ^ k) * depth, depth)
        copies.append(pltpu.make_async_copy(source, weight.at[:, pl.ds(start, depth), :], sems.at[k]))
    return copies


def activate(where_ref, x_ref, weight, first_slot, group_slots):
    slots, width, columns = weight.shape
    units = columns // 2
    x = x_ref[:, :width]
    shares = x_ref[:, width:]
    first = where_ref[0] * group_slots + first_slot
    pairs = shares.shape[1]
    place = lax.broadcasted_iota(jnp.int32, (pairs, slots * units), 0) % (pairs // 2)
    lane = lax.broadcasted_iota(jnp.int32, (pairs, slots * units), 1) // units
    spread = jnp.where(place == lane + first, 1.0, 0.0).astype(bf16)
    factor = jnp.dot(shares, spread, preferred_element_type=f32)
    parts = []
    for slot in range(slots):
        both = jnp.dot(x, weight[slot], preferred_element_type=f32)
        gate, up = both[:, :units], both[:, units:]
        act = gate / (1.0 + jnp.exp(-gate)) * up
        parts.append((act * factor[:, slot * units:(slot + 1) * units]).astype(bf16))
    return parts


def act_kernel(first_slot, group_slots, shards, where_ref, x_ref, *refs):
    sources, (act_ref, weight, sems) = refs[:shards], refs[shards:]

    @pl.when(pl.program_id(0) == 0)
    def _():
        copies = load_weights(where_ref, sources, weight, sems)
        for copy in copies:
            copy.start()
        for copy in copies:
            copy.wait()

    parts = activate(where_ref, x_ref, weight, first_slot, group_slots)
    units = parts[0].shape[1]
    for slot, part in enumerate(parts):
        act_ref[:, slot * units:(slot + 1) * units] = part


def act_block(where, x, sources, first_slot, group_slots):
    rows, wide = x.shape
    slots, depth, columns = sources[0].shape
    units = columns // 2
    shards = len(sources)
    hbm = pl.BlockSpec(memory_space=pl.ANY)
    return pl.pallas_call(
        functools.partial(act_kernel, first_slot, group_slots, shards),
        out_shape=jax.ShapeDtypeStruct((rows, slots * units), bf16),
        grid=(rows // row_tile,),
        in_specs=[pl.BlockSpec(memory_space=pltpu.SMEM), pl.BlockSpec((row_tile, wide), lambda i: (i, 0))] + [hbm] * shards,
        out_specs=pl.BlockSpec((row_tile, slots * units), lambda i: (i, 0)),
        scratch_shapes=[
            pltpu.VMEM((slots, depth * shards, columns), bf16),
            pltpu.SemaphoreType.DMA((shards,)),
        ],
        compiler_params=pltpu.CompilerParams(vmem_limit_bytes=vmem_limit),
        cost_estimate=pl.CostEstimate(
            flops=2 * rows * depth * shards * columns * slots,
            bytes_accessed=2 * (rows * wide + rows * slots * units + slots * depth * shards * columns),
            transcendentals=rows * slots * units,
        ),
        name="act_block",
    )(where, x, *sources)


def down_kernel(first_slot, group_slots, shards, earlier, where_ref, x_ref, *refs):
    acts = refs[:earlier]
    sources = refs[earlier:earlier + shards]
    down_hbm, out_ref, weight, down, act, sems = refs[earlier + shards:]

    @pl.when(pl.program_id(0) == 0)
    def _():
        copies = load_weights(where_ref, sources, weight, sems)
        copies.append(pltpu.make_async_copy(down_hbm, down, sems.at[shards]))
        for copy in copies:
            copy.start()
        for copy in copies:
            copy.wait()

    parts = activate(where_ref, x_ref, weight, first_slot, group_slots)
    units = parts[0].shape[1]
    at = 0
    for ref in acts:
        act[:, at:at + ref.shape[1]] = ref[...]
        at += ref.shape[1]
    for part in parts:
        act[:, at:at + units] = part
        at += units
    out_ref[...] = jnp.dot(act[...], down[...], preferred_element_type=f32).astype(bf16)


def down_block(where, x, acts, sources, down, first_slot, group_slots):
    rows, wide = x.shape
    slots, depth, columns = sources[0].shape
    units = columns // 2
    shards = len(sources)
    total, width = down.shape
    hbm = pl.BlockSpec(memory_space=pl.ANY)
    return pl.pallas_call(
        functools.partial(down_kernel, first_slot, group_slots, shards, len(acts)),
        out_shape=jax.ShapeDtypeStruct((rows, width), bf16),
        grid=(rows // row_tile,),
        in_specs=[pl.BlockSpec(memory_space=pltpu.SMEM), pl.BlockSpec((row_tile, wide), lambda i: (i, 0))]
        + [pl.BlockSpec((row_tile, a.shape[1]), lambda i: (i, 0)) for a in acts]
        + [hbm] * (shards + 1),
        out_specs=pl.BlockSpec((row_tile, width), lambda i: (i, 0)),
        scratch_shapes=[
            pltpu.VMEM((slots, depth * shards, columns), bf16),
            pltpu.VMEM((total, width), bf16),
            pltpu.VMEM((row_tile, total), bf16),
            pltpu.SemaphoreType.DMA((shards + 1,)),
        ],
        compiler_params=pltpu.CompilerParams(vmem_limit_bytes=vmem_limit),
        cost_estimate=pl.CostEstimate(
            flops=2 * rows * (depth * shards * columns * slots + total * width),
            bytes_accessed=2 * (rows * (wide + total + width) + slots * depth * shards * columns + total * width),
            transcendentals=rows * slots * units,
        ),
        name="down_block",
    )(where, x, *acts, *sources, down)


def plane_gather(block):
    half = block.shape[0] // 2
    a, b = block[:half], block[half:]
    a_x = swap(a, "expert", 2)
    b_y = swap(b, "expert", 4)
    a_y = swap(jnp.concatenate([a, a_x]), "expert", 4)
    b_x = swap(jnp.concatenate([b, b_y]), "expert", 2)
    mine = jnp.concatenate([a, b, a_x, b_x[:half], a_y[:half], b_y, a_y[half:], b_x[half:]])
    other = swap(mine, "expert", 1)
    return jnp.concatenate([mine, other])


def add(left, right):
    return (left.astype(f32) + right.astype(f32)).astype(bf16)


def plane_scatter(partial):
    rows, width = partial.shape
    half = width // 2
    other = swap(partial[rows // 2:], "expert", 1)
    chips = add(partial[:rows // 2], other).reshape(4, rows // 8, width)
    a, b = chips[..., :half], chips[..., half:]
    a_x = swap(jnp.stack([a[1], a[3]]), "expert", 2)
    b_y = swap(b[2:], "expert", 4)
    a_y = swap(add(a[2], a_x[1]), "expert", 4)
    b_x = swap(add(b[1], b_y[1]), "expert", 2)
    left = a[0].astype(f32) + a_x[0].astype(f32) + a_y.astype(f32)
    right = b[0].astype(f32) + b_y[0].astype(f32) + b_x.astype(f32)
    return jnp.concatenate([left, right], axis=1)


def quarter_body(
    head_outputs,
    residual,
    output_weight,
    router,
    norm_gain,
    placed_gate_up,
    placed_down,
    routes,
    replica_pick,
    placement,
    final_gain,
):
    rows, width = residual.shape
    slots, depth, columns = placed_gate_up.shape
    groups, shards = lax.axis_size("expert"), lax.axis_size("shard")
    e, s = lax.axis_index("expert"), lax.axis_index("shard")
    where = jnp.stack([e, s]).astype(jnp.int32)
    hidden_units = columns // 2
    units = hidden_units // shards

    piece = output_weight.shape[0] // groups
    own = lax.dynamic_slice_in_dim(output_weight, e * piece, piece, 0)
    pieces = jnp.stack([own] + [swap(own, "shard", k) for k in range(1, shards)])
    mine = jnp.stack([pieces] + [swap(pieces, "expert", 2 * chip) for chip in range(1, groups // 2)])
    other = swap(mine, "expert", 1)

    def quarter(k, first):
        at = (s ^ k) * units
        part = placed_gate_up[first:first + chunk_slots]
        return jnp.concatenate(
            [
                lax.dynamic_slice_in_dim(part, at, units, 2),
                lax.dynamic_slice_in_dim(part, hidden_units + at, units, 2),
            ],
            axis=2,
        )

    weights = []
    for first in range(0, slots, chunk_slots):
        weights.append([quarter(0, first)] + [swap(quarter(k, first), "shard", k) for k in range(1, shards)])

    hits = hit_table(routes, replica_pick, placement)
    spread = jnp.take(router, placement, axis=1)
    block, hidden = project(
        where, head_outputs, residual, norm_gain.reshape(1, -1),
        jnp.concatenate([spread, spread], axis=1), jnp.concatenate([hits, hits], axis=1), mine, other,
    )

    xs = [plane_gather(block if k == 0 else swap(block, "shard", k)) for k in range(shards)]

    down = placed_down.reshape(slots * units, width)
    last = len(weights) - 1
    total = hidden.astype(f32)
    acts = [[] for _ in xs]
    for chunk in range(last):
        for k in range(shards):
            acts[k].append(act_block(where, xs[k], weights[chunk], chunk * chunk_slots, slots))
    sums = []
    for k in list(range(1, shards)) + [0]:
        partial = down_block(where, xs[k], acts[k], weights[last], down, last * chunk_slots, slots)
        mine_sum = plane_scatter(partial)
        sums.append(swap(mine_sum.astype(bf16), "shard", k).astype(f32) if k else mine_sum)
    for part in sums:
        total = total + part
    return rms_scale(total, final_gain).astype(bf16)


def choose_slots(routes, replica_pick, placement, experts):
    labels = jnp.arange(experts, dtype=jnp.int32)
    holder_mask = (placement[None, :] == labels[:, None]).astype(jnp.int32)
    before = jnp.cumsum(holder_mask, axis=1) - holder_mask
    copies = jnp.sum(holder_mask, axis=1)
    places = jnp.arange(placement.shape[0], dtype=jnp.int32)
    route_hits = (routes[..., None] == labels).astype(jnp.int32)
    held_count = jnp.sum(route_hits * copies, axis=-1)
    wanted = replica_pick % held_count
    chosen = jnp.zeros(routes.shape, jnp.int32)
    for replica in range(most_copies):
        column = jnp.sum(
            holder_mask * (before == replica).astype(jnp.int32) * places[None, :], axis=1
        )
        candidate = jnp.sum(route_hits * column, axis=-1)
        chosen = jnp.where(wanted == replica, candidate, chosen)
    return chosen


def padded_experts(inbound, gate_up, down_proj):
    sources, slot_count, slot_depth, model_width = inbound.shape
    per_source = slot_count * slot_depth
    upper_bound = max(1, 1024 // per_source)
    power_two = 1 << upper_bound.bit_length() - 1
    group_size = math.gcd(sources, power_two)
    stacked = inbound.reshape(
        sources // group_size, group_size, slot_count, slot_depth, model_width
    )
    hidden_units = down_proj.shape[1]

    def apply_block(block_part):
        both_parts = jnp.einsum(
            "bjmd,jdf->bjmf", block_part, gate_up, preferred_element_type=jnp.float32
        )
        activated = (
            jax.nn.silu(both_parts[..., :hidden_units]) * both_parts[..., hidden_units:]
        ).astype(jnp.bfloat16)
        return jnp.einsum(
            "bjmf,jfd->bjmd", activated, down_proj, preferred_element_type=jnp.float32
        ).astype(jnp.bfloat16)

    return lax.map(apply_block, stacked).reshape(inbound.shape)


def body(
    head_outputs,
    residual,
    output_weight,
    router,
    norm_gain,
    placed_gate_up,
    placed_down,
    routes,
    replica_pick,
    placement,
    final_gain,
):
    row_count, model_width = residual.shape
    route_count = routes.shape[1]
    experts = router.shape[1]
    place_count = placement.shape[0]
    groups = lax.axis_size("expert")
    slot_count = place_count // groups
    capacity = CAP
    projected = jnp.dot(
        head_outputs,
        lax.all_gather(output_weight, "shard", axis=0, tiled=True),
        preferred_element_type=jnp.float32,
    )
    hidden = (residual.astype(jnp.float32) + projected).astype(jnp.bfloat16)
    hidden_wide = hidden.astype(jnp.float32)
    normed = rms_scale(hidden_wide, norm_gain).astype(jnp.bfloat16)
    logits = jnp.dot(normed, router, preferred_element_type=jnp.float32)
    labels = jnp.arange(experts, dtype=jnp.int32)
    selector = (routes[..., None] == labels).astype(jnp.float32)
    chosen_logits = jnp.sum(selector * logits[:, None, :], axis=-1)
    raised = jnp.exp(chosen_logits)
    route_weight = raised / jnp.sum(raised, axis=-1, keepdims=True)
    slot_ids = choose_slots(routes, replica_pick, placement, experts).reshape(-1)
    slot_hits = (slot_ids[:, None] == jnp.arange(place_count, dtype=jnp.int32)).astype(jnp.int32)
    slot_rank = jnp.sum((jnp.cumsum(slot_hits, axis=0) - slot_hits) * slot_hits, axis=1)
    copies_out = jnp.repeat(normed, route_count, axis=0)
    gate_up, down_proj = (
        lax.all_gather(placed_gate_up, "shard", axis=1, tiled=True),
        lax.all_gather(placed_down, "shard", axis=1, tiled=True),
    )
    buffer_index = slot_ids * capacity + slot_rank
    outbound = (
        jnp.zeros((place_count * capacity, model_width), jnp.bfloat16)
        .at[buffer_index]
        .set(copies_out)
    )
    inbound = lax.all_to_all(
        outbound.reshape(groups, slot_count * capacity, model_width),
        "expert",
        split_axis=0,
        concat_axis=0,
        tiled=True,
    )
    inbound = inbound.reshape(groups, slot_count, capacity, model_width)
    answers = padded_experts(inbound, gate_up, down_proj)
    returned = lax.all_to_all(
        answers.reshape(groups, slot_count * capacity, model_width),
        "expert",
        split_axis=0,
        concat_axis=0,
        tiled=True,
    )
    returned = returned.reshape(place_count * capacity, model_width)
    gathered = returned[buffer_index].reshape(row_count, route_count, model_width)
    mixture = jnp.sum(route_weight[..., None] * gathered.astype(jnp.float32), axis=1)
    return rms_scale(hidden_wide + mixture, final_gain).astype(jnp.bfloat16)


def solution(mesh):
    by_quarters = mesh.shape["expert"] == 8 and mesh.shape["shard"] == 4
    return jax.shard_map(
        quarter_body if by_quarters else body,
        mesh=mesh,
        in_specs=(
            P(("expert", "shard"), None),
            P(("expert", "shard"), None),
            P("shard", None),
            P(),
            P(),
            P("expert", "shard", None),
            P("expert", "shard", None),
            P(("expert", "shard"), None),
            P(("expert", "shard"), None),
            P(),
            P(),
        ),
        out_specs=P(("expert", "shard"), None),
        check_vma=False,
    )
```

```python
import functools
import math

import jax
import jax.numpy as jnp
from jax import lax
from jax.experimental import pallas as pl
from jax.experimental.pallas import tpu as pltpu
from jax.sharding import PartitionSpec as P

CAP = 48


eps_norm = 1e-06
most_copies = 3


def rms_scale(values, scale_gain):
    mean_square = jnp.mean(values * values, axis=-1, keepdims=True)
    return values * lax.rsqrt(mean_square + eps_norm) * scale_gain


bf16 = jnp.bfloat16
f32 = jnp.float32
vmem_limit = 62 * 1024 * 1024
chunks = ((0, 4), (4, 2), (6, 2))
any_space = pl.BlockSpec(memory_space=pl.ANY)
in_vmem = pl.BlockSpec(memory_space=pltpu.VMEM)
in_smem = pl.BlockSpec(memory_space=pltpu.SMEM)


def swap(value, axis, bits):
    size = lax.axis_size(axis)
    return lax.ppermute(value, axis, [(i, i ^ bits) for i in range(size)])


def hit_table(routes_ref, picks_ref, column_ref, row_ref):
    tokens, top = routes_ref.shape
    places, lanes = column_ref.shape[0], row_ref.shape[1]
    row = row_ref[...]
    same = column_ref[...] == row
    q = lax.broadcasted_iota(jnp.int32, (places, lanes), 0)
    p = lax.broadcasted_iota(jnp.int32, (places, lanes), 1) % places
    copies = jnp.sum(jnp.where(same, 1, 0), axis=0, keepdims=True)
    rank = jnp.sum(jnp.where(same & (q < p), 1, 0), axis=0, keepdims=True)
    hits = jnp.zeros((tokens, lanes), f32)
    for k in range(top):
        route, pick = routes_ref[:, k:k + 1], picks_ref[:, k:k + 1]
        wanted = jnp.zeros((tokens, lanes), jnp.int32)
        for count in range(2, most_copies + 1):
            wanted = jnp.where(copies == count, lax.rem(pick, jnp.full_like(pick, count)), wanted)
        hits = jnp.where((route == row) & (wanted == rank), 1.0, hits)
    return hits


def project_kernel(
    where_ref, heads_ref, residual_ref, gain_ref, router_ref, routes_ref, picks_ref, column_ref, row_ref, *refs
):
    pieces, (rows_ref, hidden_ref, weight, sems) = refs[:-4], refs[-4:]
    e = where_ref[0]
    s = where_ref[1]
    chips = len(pieces) // 2
    shards, piece, _ = pieces[0].shape
    depth = weight.shape[0] // shards
    copies = []
    for core in range(2):
        for chip in range(chips):
            for k in range(shards):
                start = pl.multiple_of((s ^ k) * depth + (e ^ (2 * chip + core)) * piece, piece)
                copies.append(
                    pltpu.make_async_copy(
                        pieces[core * chips + chip].at[k],
                        weight.at[pl.ds(start, piece), :],
                        sems.at[(core * chips + chip) * shards + k],
                    )
                )
    for copy in copies:
        copy.start()
    hits = hit_table(routes_ref, picks_ref, column_ref, row_ref)
    experts = router_ref.shape[1]
    chosen = lax.broadcasted_iota(jnp.int32, (experts, row_ref.shape[1]), 0) == row_ref[...]
    router = jnp.dot(router_ref[...], jnp.where(chosen, 1.0, 0.0).astype(bf16), preferred_element_type=f32).astype(bf16)
    for copy in copies:
        copy.wait()
    projected = jnp.dot(heads_ref[...], weight[...], preferred_element_type=f32)
    hidden = (residual_ref[...].astype(f32) + projected).astype(bf16)
    hidden_ref[...] = hidden
    normed = rms_scale(hidden.astype(f32), gain_ref[...]).astype(bf16)
    width = normed.shape[1]
    rows_ref[:, :width] = normed
    logits = jnp.dot(normed, router, preferred_element_type=f32)
    places = logits.shape[1] // 2
    raised = jnp.where(hits > 0, jnp.exp(logits), 0.0)
    total = jnp.sum(raised, axis=-1, keepdims=True) * 0.5
    share = raised / total
    high = share.astype(bf16)
    low = (share - high.astype(f32)).astype(bf16)
    lane = lax.broadcasted_iota(jnp.int32, share.shape, 1)
    rows_ref[:, width:] = jnp.where(lane < places, high.astype(f32), low.astype(f32)).astype(bf16)


def project(where, heads, residual, gain, router, routes, picks, placement, pieces):
    rows, width = residual.shape
    pairs = 2 * placement.shape[0]
    count = len(pieces) * pieces[0].shape[0]
    return pl.pallas_call(
        project_kernel,
        out_shape=(
            jax.ShapeDtypeStruct((rows, width + pairs), bf16),
            jax.ShapeDtypeStruct((rows, width), bf16),
        ),
        in_specs=[in_smem] + [in_vmem] * 8 + [any_space] * len(pieces),
        out_specs=(in_vmem, in_vmem),
        scratch_shapes=[
            pltpu.VMEM((width, width), bf16),
            pltpu.SemaphoreType.DMA((count,)),
        ],
        compiler_params=pltpu.CompilerParams(vmem_limit_bytes=vmem_limit),
        cost_estimate=pl.CostEstimate(
            flops=2 * rows * width * width, bytes_accessed=3 * width * width, transcendentals=rows * 128
        ),
        name="project",
    )(
        where, heads, residual, gain.reshape(1, -1), router, routes, picks,
        placement.reshape(-1, 1), jnp.tile(placement, 2).reshape(1, -1), *pieces,
    )


def quarters_kernel(weights_ref, send_ref):
    shards, _, columns = send_ref.shape
    units = columns // 2
    for q in range(shards):
        for part in range(2):
            at = (part * shards + q) * units
            send_ref[q, :, part * units:(part + 1) * units] = weights_ref[0, :, at:at + units]


def quarters(weights, first, slots, shards):
    _, depth, columns = weights.shape
    part = columns // shards
    return pl.pallas_call(
        quarters_kernel,
        out_shape=jax.ShapeDtypeStruct((shards, depth, part * slots), bf16),
        grid=(slots,),
        in_specs=[pl.BlockSpec((1, depth, columns), lambda i: (first + i, 0, 0))],
        out_specs=pl.BlockSpec((shards, depth, part), lambda i: (0, 0, i)),
        compiler_params=pltpu.CompilerParams(vmem_limit_bytes=vmem_limit),
        cost_estimate=pl.CostEstimate(flops=0, bytes_accessed=4 * depth * columns * slots, transcendentals=0),
        name="quarters",
    )(weights)


class Loads:
    def __init__(self, sems):
        self.sems = sems
        self.used = 0
        self.waiting = {}

    def start(self, name, source, target):
        copy = pltpu.make_async_copy(source, target, self.sems.at[self.used])
        copy.start()
        self.used += 1
        self.waiting.setdefault(name, []).append(copy)

    def wait(self, name):
        for copy in self.waiting.pop(name, []):
            copy.wait()


def load_weights(loads, name, source, weight):
    shards, depth, _ = source.shape
    for q in range(shards):
        loads.start(name, source.at[q], weight.at[pl.ds(q * depth, depth), :])


def activate(where_ref, x, shares, weight, first_slot, group_slots):
    units = shares.shape[1]
    columns = 2 * units
    slots = weight.shape[1] // columns
    first = where_ref[0] * group_slots + first_slot
    pairs = shares.shape[1]
    place = lax.broadcasted_iota(jnp.int32, (pairs, slots * units), 0) % (pairs // 2)
    lane = lax.broadcasted_iota(jnp.int32, (pairs, slots * units), 1) // units
    spread = jnp.where(place == lane + first, 1.0, 0.0).astype(bf16)
    factor = jnp.dot(shares, spread, preferred_element_type=f32)
    both = jnp.dot(x, weight, preferred_element_type=f32)
    parts = []
    for slot in range(slots):
        gate = both[:, slot * columns:slot * columns + units]
        up = both[:, slot * columns + units:(slot + 1) * columns]
        act = gate / (1.0 + jnp.exp(-gate)) * up
        parts.append((act * factor[:, slot * units:(slot + 1) * units]).astype(bf16))
    return parts


def slots_kernel(slot_sets, group_slots, group_sizes, has_sums, where_ref, *refs):
    refs = list(refs)

    def take(count):
        taken, refs[:] = refs[:count], refs[count:]
        return taken

    groups = len(group_sizes)
    blocks = [take(size) for size in group_sizes]
    sources = take(len(slot_sets))
    (down_hbm,) = take(1)
    earlier = take(groups) if has_sums else []
    outs = take(groups)
    x, total = take(2)
    weights = take(len(slot_sets))
    down, sems = take(2)
    width = weights[0].shape[0]
    units = x.shape[2] - width
    loads = Loads(sems)

    def load_group(group):
        at = 0
        for ref in blocks[group]:
            loads.start(f"x{group}", ref, x.at[group, pl.ds(at, ref.shape[0]), :])
            at += ref.shape[0]

    load_weights(loads, "w0", sources[0], weights[0])
    load_group(0)
    loads.wait("w0")
    for group in range(groups):
        loads.wait(f"x{group}")
        if group == 0:
            for i in range(1, len(slot_sets)):
                load_weights(loads, f"w{i}", sources[i], weights[i])
            at = 0
            for first, count in slot_sets:
                rows = pl.ds(first * units, count * units)
                loads.start("down", down_hbm.at[rows, :], down.at[pl.ds(at * units, count * units), :])
                at += count
            for later in range(groups):
                if later:
                    load_group(later)
                if has_sums:
                    loads.start(f"sum{later}", earlier[later], total.at[later])
        parts = []
        for i, (first, _) in enumerate(slot_sets):
            loads.wait(f"w{i}")
            parts += activate(where_ref, x[group, :, :width], x[group, :, width:], weights[i][...], first, group_slots)
        loads.wait("down")
        added = jnp.dot(jnp.concatenate(parts, axis=1), down[...], preferred_element_type=f32)
        if has_sums:
            loads.wait(f"sum{group}")
            added = added + total[group].astype(f32)
        total[group] = added.astype(bf16)
        loads.start(f"out{group}", total.at[group], outs[group])
    for group in range(groups):
        loads.wait(f"out{group}")


def slots_block(where, groups, sources, slot_sets, down, earlier, group_slots):
    sizes = tuple(len(blocks) for blocks in groups)
    rows = sum(block.shape[0] for block in groups[0])
    wide = groups[0][0].shape[1]
    shards, depth, _ = sources[0].shape
    width = down.shape[1]
    columns = sum(source.shape[2] for source in sources)
    blocks = [block for group in groups for block in group]
    return pl.pallas_call(
        functools.partial(slots_kernel, slot_sets, group_slots, sizes, bool(earlier)),
        out_shape=[jax.ShapeDtypeStruct((rows, width), bf16)] * len(groups),
        in_specs=[in_smem] + [any_space] * (len(blocks) + len(sources) + 1 + len(earlier)),
        out_specs=[any_space] * len(groups),
        scratch_shapes=[
            pltpu.VMEM((len(groups), rows, wide), bf16),
            pltpu.VMEM((len(groups), rows, width), bf16),
        ]
        + [pltpu.VMEM((depth * shards, source.shape[2]), bf16) for source in sources]
        + [
            pltpu.VMEM((columns // 2, width), bf16),
            pltpu.SemaphoreType.DMA((len(blocks) + (shards + 1) * len(sources) + 2 * len(groups),)),
        ],
        compiler_params=pltpu.CompilerParams(vmem_limit_bytes=vmem_limit),
        cost_estimate=pl.CostEstimate(
            flops=2 * rows * len(groups) * columns * (depth * shards + width // 2),
            bytes_accessed=2 * (rows * len(groups) * (wide + 2 * width) + columns * (depth * shards + width // 2)),
            transcendentals=rows * len(groups) * columns // 2,
        ),
        name="slots_block",
    )(where, *blocks, *sources, down, *earlier)


def after(value, *events):
    return lax.optimization_barrier((value, *events))[0]


def chip_gather(block):
    return [block] + [swap(block, "expert", bits) for bits in (2, 4, 6)]


def core_gather(chips):
    return chips + [swap(chip, "expert", 1) for chip in chips]


def stage(*values):
    return lax.optimization_barrier(values)


def add(left, right):
    return (left.astype(f32) + right.astype(f32)).astype(bf16)


def quarter_body(
    head_outputs,
    residual,
    output_weight,
    router,
    norm_gain,
    placed_gate_up,
    placed_down,
    routes,
    replica_pick,
    placement,
    final_gain,
):
    rows, width = residual.shape
    slots, depth, columns = placed_gate_up.shape
    devices, shards = lax.axis_size("expert"), lax.axis_size("shard")
    e, s = lax.axis_index("expert"), lax.axis_index("shard")
    where = jnp.stack([e, s]).astype(jnp.int32)
    hidden_units = columns // 2
    units = hidden_units // shards

    piece = output_weight.shape[0] // devices
    own = lax.dynamic_slice_in_dim(output_weight, e * piece, piece, 0)
    over_z = jnp.stack([own] + [swap(own, "shard", k) for k in range(1, shards)])

    sends = [quarters(placed_gate_up, first, count, shards) for first, count in chunks]

    def exchange(send):
        return lax.all_to_all(send, "shard", split_axis=0, concat_axis=0, tiled=True)

    over_z, send = stage(over_z, sends[0])
    weights = [exchange(send)]
    pieces = core_gather(chip_gather(over_z))
    block, hidden = project(where, head_outputs, residual, norm_gain, router, routes, replica_pick, placement, pieces)

    inner = (s == 1) | (s == 2)
    cross = [(1, 2), (2, 1)]
    outward = [(1, 0), (2, 3)]

    own_chips = chip_gather(block)
    near = swap(block, "shard", 1)
    first_in = lax.ppermute(block, "shard", cross)
    near, first_in, send, *own_chips = stage(near, first_in, sends[1], *own_chips)

    near_chips = chip_gather(near)
    first_out = lax.ppermute(first_in, "shard", outward)
    second_in = lax.ppermute(near, "shard", cross)
    own_all = core_gather(own_chips)
    first_out, second_in, weights[0], *rest = stage(first_out, second_in, weights[0], *near_chips, *own_all)
    near_chips, own_all = rest[:4], rest[4:]

    weights.append(exchange(after(send, weights[0])))
    far_a = jnp.where(inner, first_in, first_out)
    far_a_chips = chip_gather(far_a)
    second_out = lax.ppermute(second_in, "shard", outward)
    near_all = core_gather(near_chips)
    second_out, send, *rest = stage(second_out, sends[2], *far_a_chips, *near_all)
    far_a_chips, near_all = rest[:4], rest[4:]

    far_b = jnp.where(inner, second_in, second_out)
    far_b_chips = chip_gather(far_b)
    far_a_all = core_gather(far_a_chips)
    weights[1], *rest = stage(weights[1], *far_b_chips, *far_a_all)
    far_b_chips, far_a_all = rest[:4], rest[4:]

    weights.append(exchange(after(send, weights[1])))
    far_b_all = core_gather(far_b_chips)

    down = placed_down.reshape(slots * units, width)
    groups = [[chips[4:], chips[:4]] for chips in (own_all, near_all, far_a_all, far_b_all)]
    before = slots_block(where, groups[0] + groups[1], weights[:2], chunks[:2], down, [], slots)
    before += slots_block(where, groups[2] + groups[3], weights[:2], chunks[:2], down, [], slots)
    before = stage(*before)

    order = (3, 2, 1, 0)
    half = width // 2
    chips, halves, sums = {}, {}, {}
    for step, k in enumerate(order):
        events = []
        if step >= 2:
            events.append(chips[order[step - 2]])
        if step >= 3:
            events.append(halves[order[step - 3]])
        earlier = [after(before[2 * k], *events), before[2 * k + 1]]
        other, own = slots_block(where, groups[k], weights[2:], chunks[2:], down, earlier, slots)
        chip = add(own, swap(other, "expert", 1)).reshape(devices // 2, rows, width)
        a, b = chip[..., :half], chip[..., half:]
        a_x = swap(jnp.stack([a[1], a[3]]), "expert", 2)
        b_y = swap(b[2:], "expert", 4)
        a_y = swap(add(a[2], a_x[1]), "expert", 4)
        b_x = swap(add(b[1], b_y[1]), "expert", 2)
        left = a[0].astype(f32) + a_x[0].astype(f32) + a_y.astype(f32)
        right = b[0].astype(f32) + b_y[0].astype(f32) + b_x.astype(f32)
        chips[k] = chip
        halves[k] = (a_x, b_y)
        sums[k] = jnp.concatenate([left, right], axis=1)
    sent = [
        swap(sums[1].astype(bf16), "shard", 1),
        swap(jnp.where(inner, sums[3], sums[2]).astype(bf16), "shard", 2),
        swap(jnp.where(inner, sums[2], sums[3]).astype(bf16), "shard", 3),
    ]
    total = hidden.astype(f32) + sums[0]
    for part in sent:
        total = total + part.astype(f32)
    return rms_scale(total, final_gain).astype(bf16)


def choose_slots(routes, replica_pick, placement, experts):
    labels = jnp.arange(experts, dtype=jnp.int32)
    holder_mask = (placement[None, :] == labels[:, None]).astype(jnp.int32)
    before = jnp.cumsum(holder_mask, axis=1) - holder_mask
    copies = jnp.sum(holder_mask, axis=1)
    places = jnp.arange(placement.shape[0], dtype=jnp.int32)
    route_hits = (routes[..., None] == labels).astype(jnp.int32)
    held_count = jnp.sum(route_hits * copies, axis=-1)
    wanted = replica_pick % held_count
    chosen = jnp.zeros(routes.shape, jnp.int32)
    for replica in range(most_copies):
        column = jnp.sum(
            holder_mask * (before == replica).astype(jnp.int32) * places[None, :], axis=1
        )
        candidate = jnp.sum(route_hits * column, axis=-1)
        chosen = jnp.where(wanted == replica, candidate, chosen)
    return chosen


def padded_experts(inbound, gate_up, down_proj):
    sources, slot_count, slot_depth, model_width = inbound.shape
    per_source = slot_count * slot_depth
    upper_bound = max(1, 1024 // per_source)
    power_two = 1 << upper_bound.bit_length() - 1
    group_size = math.gcd(sources, power_two)
    stacked = inbound.reshape(
        sources // group_size, group_size, slot_count, slot_depth, model_width
    )
    hidden_units = down_proj.shape[1]

    def apply_block(block_part):
        both_parts = jnp.einsum(
            "bjmd,jdf->bjmf", block_part, gate_up, preferred_element_type=jnp.float32
        )
        activated = (
            jax.nn.silu(both_parts[..., :hidden_units]) * both_parts[..., hidden_units:]
        ).astype(jnp.bfloat16)
        return jnp.einsum(
            "bjmf,jfd->bjmd", activated, down_proj, preferred_element_type=jnp.float32
        ).astype(jnp.bfloat16)

    return lax.map(apply_block, stacked).reshape(inbound.shape)


def body(
    head_outputs,
    residual,
    output_weight,
    router,
    norm_gain,
    placed_gate_up,
    placed_down,
    routes,
    replica_pick,
    placement,
    final_gain,
):
    row_count, model_width = residual.shape
    route_count = routes.shape[1]
    experts = router.shape[1]
    place_count = placement.shape[0]
    groups = lax.axis_size("expert")
    slot_count = place_count // groups
    capacity = CAP
    projected = jnp.dot(
        head_outputs,
        lax.all_gather(output_weight, "shard", axis=0, tiled=True),
        preferred_element_type=jnp.float32,
    )
    hidden = (residual.astype(jnp.float32) + projected).astype(jnp.bfloat16)
    hidden_wide = hidden.astype(jnp.float32)
    normed = rms_scale(hidden_wide, norm_gain).astype(jnp.bfloat16)
    logits = jnp.dot(normed, router, preferred_element_type=jnp.float32)
    labels = jnp.arange(experts, dtype=jnp.int32)
    selector = (routes[..., None] == labels).astype(jnp.float32)
    chosen_logits = jnp.sum(selector * logits[:, None, :], axis=-1)
    raised = jnp.exp(chosen_logits)
    route_weight = raised / jnp.sum(raised, axis=-1, keepdims=True)
    slot_ids = choose_slots(routes, replica_pick, placement, experts).reshape(-1)
    slot_hits = (slot_ids[:, None] == jnp.arange(place_count, dtype=jnp.int32)).astype(jnp.int32)
    slot_rank = jnp.sum((jnp.cumsum(slot_hits, axis=0) - slot_hits) * slot_hits, axis=1)
    copies_out = jnp.repeat(normed, route_count, axis=0)
    gate_up, down_proj = (
        lax.all_gather(placed_gate_up, "shard", axis=1, tiled=True),
        lax.all_gather(placed_down, "shard", axis=1, tiled=True),
    )
    buffer_index = slot_ids * capacity + slot_rank
    outbound = (
        jnp.zeros((place_count * capacity, model_width), jnp.bfloat16)
        .at[buffer_index]
        .set(copies_out)
    )
    inbound = lax.all_to_all(
        outbound.reshape(groups, slot_count * capacity, model_width),
        "expert",
        split_axis=0,
        concat_axis=0,
        tiled=True,
    )
    inbound = inbound.reshape(groups, slot_count, capacity, model_width)
    answers = padded_experts(inbound, gate_up, down_proj)
    returned = lax.all_to_all(
        answers.reshape(groups, slot_count * capacity, model_width),
        "expert",
        split_axis=0,
        concat_axis=0,
        tiled=True,
    )
    returned = returned.reshape(place_count * capacity, model_width)
    gathered = returned[buffer_index].reshape(row_count, route_count, model_width)
    mixture = jnp.sum(route_weight[..., None] * gathered.astype(jnp.float32), axis=1)
    return rms_scale(hidden_wide + mixture, final_gain).astype(jnp.bfloat16)


def solution(mesh):
    by_quarters = mesh.shape["expert"] == 8 and mesh.shape["shard"] == 4
    return jax.shard_map(
        quarter_body if by_quarters else body,
        mesh=mesh,
        in_specs=(
            P(("expert", "shard"), None),
            P(("expert", "shard"), None),
            P("shard", None),
            P(),
            P(),
            P("expert", "shard", None),
            P("expert", "shard", None),
            P(("expert", "shard"), None),
            P(("expert", "shard"), None),
            P(),
            P(),
        ),
        out_specs=P(("expert", "shard"), None),
        check_vma=False,
    )
```

```python
import functools
import math

import jax
import jax.numpy as jnp
from jax import lax
from jax.experimental import pallas as pl
from jax.experimental.pallas import tpu as pltpu
from jax.sharding import PartitionSpec as P

CAP = 48


eps_norm = 1e-06
most_copies = 3


def rms_scale(values, scale_gain):
    mean_square = jnp.mean(values * values, axis=-1, keepdims=True)
    return values * lax.rsqrt(mean_square + eps_norm) * scale_gain


bf16 = jnp.bfloat16
f32 = jnp.float32
vmem_limit = 62 * 1024 * 1024
tile_rows = 512
chunks = ((0, 3), (3, 3), (6, 2))
any_space = pl.BlockSpec(memory_space=pl.ANY)
in_vmem = pl.BlockSpec(memory_space=pltpu.VMEM)
in_smem = pl.BlockSpec(memory_space=pltpu.SMEM)


def swap(value, axis, bits):
    size = lax.axis_size(axis)
    return lax.ppermute(value, axis, [(i, i ^ bits) for i in range(size)])


def hit_table(routes, picks, column, row, places):
    lanes = row.shape[1]
    same = column == row
    q = lax.broadcasted_iota(jnp.int32, same.shape, 0)
    p = lax.broadcasted_iota(jnp.int32, same.shape, 1) % places
    copies = jnp.sum(jnp.where(same & (q < places), 1.0, 0.0), axis=0, keepdims=True)
    rank = jnp.sum(jnp.where(same & (q < p), 1.0, 0.0), axis=0, keepdims=True)
    routes = jnp.transpose(routes.astype(f32))
    rests = [jnp.transpose(lax.rem(picks, jnp.full_like(picks, count)).astype(f32)) for count in range(2, most_copies + 1)]
    hits = jnp.zeros((routes.shape[0], lanes), f32)
    for k in range(routes.shape[1]):
        wanted = jnp.zeros(hits.shape, f32)
        for count, rest in enumerate(rests, 2):
            wanted = jnp.where(copies == count, rest[:, k:k + 1], wanted)
        hits = jnp.where((routes[:, k:k + 1] == row) & (wanted == rank), 1.0, hits)
    return hits


def quarters_kernel(weights_ref, send_ref):
    shards, _, columns = send_ref.shape
    units = columns // 2
    for q in range(shards):
        for part in range(2):
            at = (part * shards + q) * units
            send_ref[q, :, part * units:(part + 1) * units] = weights_ref[0, :, at:at + units]


def quarters(weights, first, slots, shards):
    _, depth, columns = weights.shape
    part = columns // shards
    return pl.pallas_call(
        quarters_kernel,
        out_shape=jax.ShapeDtypeStruct((shards, depth, part * slots), bf16),
        grid=(slots,),
        in_specs=[pl.BlockSpec((1, depth, columns), lambda i: (first + i, 0, 0))],
        out_specs=pl.BlockSpec((shards, depth, part), lambda i: (0, 0, i)),
        compiler_params=pltpu.CompilerParams(vmem_limit_bytes=vmem_limit),
        cost_estimate=pl.CostEstimate(flops=0, bytes_accessed=4 * depth * columns * slots, transcendentals=0),
        name="quarters",
    )(weights)


class Loads:
    def __init__(self, sems):
        self.sems = sems
        self.used = 0
        self.waiting = {}

    def start(self, name, source, target):
        copy = pltpu.make_async_copy(source, target, self.sems.at[self.used])
        copy.start()
        self.used += 1
        self.waiting.setdefault(name, []).append(copy)

    def wait(self, name):
        for copy in self.waiting.pop(name, []):
            copy.wait()


def project_kernel(
    where_ref, heads_hbm, residual_hbm, gain_hbm, router_hbm, routes_hbm, picks_hbm, experts_hbm, *refs
):
    pieces = refs[:-11]
    rows_ref, hidden_ref, weight, heads_ref, residual_ref, gain_ref, router_ref = refs[-11:-4]
    routes_ref, picks_ref, experts_ref, sems = refs[-4:]
    e = where_ref[0]
    s = where_ref[1]
    chips = len(pieces) // 2
    shards, piece, _ = pieces[0].shape
    depth = weight.shape[0] // shards
    loads = Loads(sems)
    for source, target in (
        (routes_hbm, routes_ref), (picks_hbm, picks_ref), (experts_hbm, experts_ref), (router_hbm, router_ref),
    ):
        loads.start("routing", source, target)
    for core in range(2):
        for chip in range(chips):
            for k in range(shards):
                start = pl.multiple_of((s ^ k) * depth + (e ^ (2 * chip + core)) * piece, piece)
                loads.start("weight", pieces[core * chips + chip].at[k], weight.at[pl.ds(start, piece), :])
    for source, target in ((heads_hbm, heads_ref), (residual_hbm, residual_ref), (gain_hbm, gain_ref)):
        loads.start("weight", source, target)
    loads.wait("routing")
    places = experts_ref.shape[1]
    row = experts_ref[...].astype(f32)
    row = jnp.concatenate([row, row], axis=1)
    column = jnp.transpose(jnp.broadcast_to(row, (row.shape[1], row.shape[1])))
    hits = hit_table(routes_ref[...], picks_ref[...], column, row, places)
    count = router_ref.shape[0]
    label = lax.broadcasted_iota(jnp.int32, (row.shape[1], count), 1).astype(f32)
    chosen = jnp.where(column[:, :count] == label, 1.0, 0.0).astype(bf16)
    router = jnp.dot(chosen, router_ref[...], preferred_element_type=f32).astype(bf16)
    loads.wait("weight")
    projected = jnp.dot(heads_ref[...], weight[...], preferred_element_type=f32)
    hidden = (residual_ref[...].astype(f32) + projected).astype(bf16)
    hidden_ref[...] = hidden
    normed = rms_scale(hidden.astype(f32), gain_ref[...]).astype(bf16)
    width = normed.shape[1]
    rows_ref[:, :width] = normed
    logits = lax.dot_general(normed, router, (((1,), (1,)), ((), ())), preferred_element_type=f32)
    raised = jnp.where(hits > 0, jnp.exp(logits), 0.0)
    total = jnp.sum(raised, axis=-1, keepdims=True) * 0.5
    share = raised / total
    high = share.astype(bf16)
    low = (share - high.astype(f32)).astype(bf16)
    lane = lax.broadcasted_iota(jnp.int32, share.shape, 1)
    rows_ref[:, width:] = jnp.where(lane < places, high.astype(f32), low.astype(f32)).astype(bf16)


def project(where, heads, residual, gain, router, routes, picks, placement, pieces):
    rows, width = residual.shape
    pairs = 2 * placement.shape[0]
    places = placement.shape[0]
    operands = (
        heads, residual, gain.reshape(1, -1), router.T, routes.T, picks.T, placement.reshape(1, -1), *pieces,
    )
    count = len(operands) + len(pieces) * (pieces[0].shape[0] - 1)
    return pl.pallas_call(
        project_kernel,
        out_shape=(
            jax.ShapeDtypeStruct((rows, width + pairs), bf16),
            jax.ShapeDtypeStruct((rows, width), bf16),
        ),
        in_specs=[in_smem] + [any_space] * len(operands),
        out_specs=(in_vmem, in_vmem),
        scratch_shapes=[
            pltpu.VMEM((width, width), bf16),
            pltpu.VMEM((rows, width), bf16),
            pltpu.VMEM((rows, width), bf16),
            pltpu.VMEM((1, width), f32),
            pltpu.VMEM(router.shape[::-1], bf16),
            pltpu.VMEM(routes.shape[::-1], jnp.int32),
            pltpu.VMEM(picks.shape[::-1], jnp.int32),
            pltpu.VMEM((1, places), jnp.int32),
            pltpu.SemaphoreType.DMA((count,)),
        ],
        compiler_params=pltpu.CompilerParams(vmem_limit_bytes=vmem_limit),
        cost_estimate=pl.CostEstimate(
            flops=2 * rows * width * width, bytes_accessed=3 * width * width, transcendentals=rows * pairs
        ),
        name="project",
    )(where, *operands)


def activate(both, shares, first, slots):
    units = shares.shape[1]
    pairs = shares.shape[1]
    place = lax.broadcasted_iota(jnp.int32, (pairs, slots * units), 0) % (pairs // 2)
    lane = lax.broadcasted_iota(jnp.int32, (pairs, slots * units), 1) // units
    spread = jnp.where(place == lane + first, 1.0, 0.0).astype(bf16)
    factor = jnp.dot(shares, spread, preferred_element_type=f32)
    parts = []
    for slot in range(slots):
        gate = both[:, 2 * slot * units:(2 * slot + 1) * units]
        up = both[:, (2 * slot + 1) * units:(2 * slot + 2) * units]
        act = gate / (1.0 + jnp.exp(-gate)) * up
        parts.append((act * factor[:, slot * units:(slot + 1) * units]).astype(bf16))
    return parts


def slots_kernel(slot_sets, group_slots, block_count, has_sums, cut, where_ref, *refs):
    refs = list(refs)

    def take(count):
        taken, refs[:] = refs[:count], refs[count:]
        return taken

    blocks = take(block_count)
    sources = take(len(slot_sets))
    downs = take(2)
    earlier = take(1)[0] if has_sums else None
    outs = take(4 if cut else 1)
    x, total, weight, down, weight_sem, x_sems, sum_sems, out_sems = refs
    tiles, tile_rows, _ = x.shape
    width = weight.shape[0]
    units = x.shape[2] - width

    at = 0
    for source in sources:
        shards, depth, columns = source.shape
        for q in range(shards):
            rows = pl.ds(q * depth, depth)
            pltpu.make_async_copy(source.at[q], weight.at[rows, pl.ds(at, columns)], weight_sem.at[0]).start()
        at += columns

    def load_tile(tile):
        at = 0
        for block in blocks:
            rows = block.shape[0]
            if at // tile_rows == tile:
                target = x.at[tile, pl.ds(at % tile_rows, rows), :]
                pltpu.make_async_copy(block, target, x_sems.at[tile]).start()
            at += rows

    load_tile(0)
    at = 0
    for flip, first, count in slot_sets:
        source, target = downs[flip].at[pl.ds(first * units, count * units), :], down.at[pl.ds(at, count * units), :]
        pltpu.make_async_copy(source, target, weight_sem.at[1]).start()
        at += count * units
    for tile in range(tiles):
        if tile:
            load_tile(tile)
        if has_sums:
            source = earlier.at[pl.ds(tile * tile_rows, tile_rows), :]
            pltpu.make_async_copy(source, total.at[tile], sum_sems.at[tile]).start()
    pltpu.make_async_copy(weight, weight, weight_sem.at[0]).wait()
    pltpu.make_async_copy(down, down, weight_sem.at[1]).wait()

    @pl.loop(0, tiles)
    def _(tile):
        pltpu.make_async_copy(x.at[tile], x.at[tile], x_sems.at[tile]).wait()
        shares = x[tile, :, width:]
        both = jnp.dot(x[tile, :, :width], weight[...], preferred_element_type=f32)
        parts, at = [], 0
        for flip, first, count in slot_sets:
            place = (where_ref[0] ^ flip) * group_slots + first
            parts += activate(both[:, at:at + 2 * count * units], shares, place, count)
            at += 2 * count * units
        added = jnp.dot(jnp.concatenate(parts, axis=1), down[...], preferred_element_type=f32)
        if has_sums:
            pltpu.make_async_copy(total.at[tile], total.at[tile], sum_sems.at[tile]).wait()
            added = added + total[tile].astype(f32)
        total[tile] = added.astype(bf16)
        if not cut:
            target = outs[0].at[pl.ds(tile * tile_rows, tile_rows), :]
            pltpu.make_async_copy(total.at[tile], target, out_sems.at[tile]).start()

    if cut:
        rows, half = blocks[0].shape[0], width // 2
        parts = block_count // 4
        copies = []
        for part in range(parts):
            place = part if cut == "ordered" else part ^ (1 - where_ref[2])
            for out, chips, column in zip(outs, ((1, 3), (2, 3), (0, 2), (0, 1)), (0, half, 0, half)):
                for i, chip in enumerate(chips):
                    tile, at = divmod((4 * part + chip) * rows, tile_rows)
                    source = total.at[tile, pl.ds(at, rows), pl.ds(column, half)]
                    target = out.at[i, place]
                    copies.append(pltpu.make_async_copy(source, target, out_sems.at[len(copies)]))
        for copy in copies:
            copy.start()
        for copy in copies:
            copy.wait()
    else:
        @pl.loop(0, tiles)
        def _(tile):
            target = outs[0].at[pl.ds(tile * tile_rows, tile_rows), :]
            pltpu.make_async_copy(total.at[tile], target, out_sems.at[tile]).wait()


def slots_block(where, blocks, sources, slot_sets, downs, earlier, group_slots, cut=None):
    rows = sum(block.shape[0] for block in blocks)
    wide = blocks[0].shape[1]
    shards, depth, _ = sources[0].shape
    width = downs[0].shape[1]
    columns = sum(source.shape[2] for source in sources)
    tiles = rows // tile_rows
    if cut:
        out_shape = [jax.ShapeDtypeStruct((2, len(blocks) // 4, blocks[0].shape[0], width // 2), bf16)] * 4
    else:
        out_shape = [jax.ShapeDtypeStruct((rows, width), bf16)]
    return pl.pallas_call(
        functools.partial(slots_kernel, slot_sets, group_slots, len(blocks), bool(earlier), cut),
        out_shape=out_shape,
        in_specs=[in_smem] + [any_space] * (len(blocks) + len(sources) + 2 + len(earlier)),
        out_specs=[any_space] * len(out_shape),
        scratch_shapes=[
            pltpu.VMEM((tiles, tile_rows, wide), bf16),
            pltpu.VMEM((tiles, tile_rows, width), bf16),
            pltpu.VMEM((depth * shards, columns), bf16),
            pltpu.VMEM((columns // 2, width), bf16),
            pltpu.SemaphoreType.DMA((2,)),
            pltpu.SemaphoreType.DMA((tiles,)),
            pltpu.SemaphoreType.DMA((tiles,)),
            pltpu.SemaphoreType.DMA((max(tiles, 2 * len(blocks)),)),
        ],
        compiler_params=pltpu.CompilerParams(vmem_limit_bytes=vmem_limit),
        cost_estimate=pl.CostEstimate(
            flops=2 * rows * columns * (depth * shards + width // 2),
            bytes_accessed=2 * (rows * (wide + 2 * width) + columns * (depth * shards + width // 2)),
            transcendentals=rows * columns // 2,
        ),
        name="slots_block",
    )(where, *blocks, *sources, *downs, *earlier)


def after(value, *events):
    return lax.optimization_barrier((value, *events))[0]


def chip_gather(block):
    return [block] + [swap(block, "expert", bits) for bits in (2, 4, 6)]


def core_gather(chips):
    return chips + [swap(chip, "expert", 1) for chip in chips]


def stage(*values):
    return lax.optimization_barrier(values)


def add(left, right):
    return (left.astype(f32) + right.astype(f32)).astype(bf16)


def quarter_body(
    head_outputs,
    residual,
    output_weight,
    router,
    norm_gain,
    placed_gate_up,
    placed_down,
    routes,
    replica_pick,
    placement,
    final_gain,
):
    rows, width = residual.shape
    slots, depth, columns = placed_gate_up.shape
    devices, shards = lax.axis_size("expert"), lax.axis_size("shard")
    e, s = lax.axis_index("expert"), lax.axis_index("shard")
    inner = (s == 1) | (s == 2)
    where = jnp.stack([e, s, inner]).astype(jnp.int32)
    hidden_units = columns // 2
    units = hidden_units // shards

    piece = output_weight.shape[0] // devices
    own = lax.dynamic_slice_in_dim(output_weight, e * piece, piece, 0)
    over_z = jnp.stack([own] + [swap(own, "shard", k) for k in range(1, shards)])

    sends = [quarters(placed_gate_up, first, count, shards) for first, count in chunks]

    def exchange(send):
        return lax.all_to_all(send, "shard", split_axis=0, concat_axis=0, tiled=True)

    over_z, send = stage(over_z, sends[0])
    weights = [exchange(send)]
    pieces = core_gather(chip_gather(over_z))
    block, hidden = project(where, head_outputs, residual, norm_gain, router, routes, replica_pick, placement, pieces)

    cross = [(1, 2), (2, 1)]
    outward = [(1, 0), (2, 3)]

    own_chips = chip_gather(block)
    near = swap(block, "shard", 1)
    first_in = lax.ppermute(block, "shard", cross)
    near, first_in, send, sends[2], *own_chips = stage(near, first_in, sends[1], sends[2], *own_chips)

    near_chips = chip_gather(near)
    first_out = lax.ppermute(first_in, "shard", outward)
    second_in = lax.ppermute(near, "shard", cross)
    first_out, second_in, weights[0], *near_chips = stage(first_out, second_in, weights[0], *near_chips)

    weights.append(exchange(after(send, weights[0])))
    far_a = jnp.where(inner, first_in, first_out)
    far_a_chips = chip_gather(far_a)
    second_out = lax.ppermute(second_in, "shard", outward)

    down = placed_down.reshape(slots * units, width)
    downs = [down, swap(after(down, near), "expert", 1)]
    others = [swap(weights[0], "expert", 1)]
    def run(blocks, which, earlier, cut=None):
        sources, sets = [], []
        for chunk in range(len(chunks))[which]:
            sources += [weights[chunk], others[chunk]]
            sets += [(0, *chunks[chunk]), (1, *chunks[chunk])]
        return slots_block(where, blocks, sources, tuple(sets), downs, earlier, slots, cut)

    (early,) = run(near_chips + own_chips, slice(0, 1), [])
    second_out, early, *far_a_chips = stage(second_out, early, *far_a_chips)

    far_b = jnp.where(inner, second_in, second_out)
    far_b_chips = chip_gather(far_b)
    weights[1], *far_b_chips = stage(weights[1], *far_b_chips)

    weights.append(exchange(after(sends[2], weights[1])))
    others.append(swap(weights[1], "expert", 1))
    (late,) = run(far_a_chips + far_b_chips, slice(0, 2), [])
    weights[2], late = stage(weights[2], late)
    others.append(swap(weights[2], "expert", 1))

    sums = {}
    far = run(far_a_chips + far_b_chips, slice(2, 3), [late], "labelled")
    far_x, far_y = swap(far[0], "expert", 2), swap(far[1], "expert", 4)
    close = run(near_chips + own_chips, slice(1, 3), [after(early, far[2])], "ordered")
    far_x, far_y, *close = stage(far_x, far_y, *close)
    close_x, close_y = swap(close[0], "expert", 2), swap(close[1], "expert", 4)
    for pair, left, right, a_x, b_y in (
        ((3, 2), far[2], far[3], far_x, far_y), ((1, 0), close[2], close[3], close_x, close_y)
    ):
        a_y = swap(add(left[1], a_x[1]), "expert", 4)
        b_x = swap(add(right[1], b_y[1]), "expert", 2)
        left = left[0].astype(f32) + a_x[0].astype(f32) + a_y.astype(f32)
        right = right[0].astype(f32) + b_y[0].astype(f32) + b_x.astype(f32)
        for i, k in enumerate(pair):
            sums[k] = jnp.concatenate([left[i], right[i]], axis=1)
    sent = [swap(sums[k].astype(bf16), "shard", k) for k in range(1, shards)]
    total = hidden.astype(f32) + sums[0]
    for part in sent:
        total = total + part.astype(f32)
    return rms_scale(total, final_gain).astype(bf16)


def choose_slots(routes, replica_pick, placement, experts):
    labels = jnp.arange(experts, dtype=jnp.int32)
    holder_mask = (placement[None, :] == labels[:, None]).astype(jnp.int32)
    before = jnp.cumsum(holder_mask, axis=1) - holder_mask
    copies = jnp.sum(holder_mask, axis=1)
    places = jnp.arange(placement.shape[0], dtype=jnp.int32)
    route_hits = (routes[..., None] == labels).astype(jnp.int32)
    held_count = jnp.sum(route_hits * copies, axis=-1)
    wanted = replica_pick % held_count
    chosen = jnp.zeros(routes.shape, jnp.int32)
    for replica in range(most_copies):
        column = jnp.sum(
            holder_mask * (before == replica).astype(jnp.int32) * places[None, :], axis=1
        )
        candidate = jnp.sum(route_hits * column, axis=-1)
        chosen = jnp.where(wanted == replica, candidate, chosen)
    return chosen


def padded_experts(inbound, gate_up, down_proj):
    sources, slot_count, slot_depth, model_width = inbound.shape
    per_source = slot_count * slot_depth
    upper_bound = max(1, 1024 // per_source)
    power_two = 1 << upper_bound.bit_length() - 1
    group_size = math.gcd(sources, power_two)
    stacked = inbound.reshape(
        sources // group_size, group_size, slot_count, slot_depth, model_width
    )
    hidden_units = down_proj.shape[1]

    def apply_block(block_part):
        both_parts = jnp.einsum(
            "bjmd,jdf->bjmf", block_part, gate_up, preferred_element_type=jnp.float32
        )
        activated = (
            jax.nn.silu(both_parts[..., :hidden_units]) * both_parts[..., hidden_units:]
        ).astype(jnp.bfloat16)
        return jnp.einsum(
            "bjmf,jfd->bjmd", activated, down_proj, preferred_element_type=jnp.float32
        ).astype(jnp.bfloat16)

    return lax.map(apply_block, stacked).reshape(inbound.shape)


def body(
    head_outputs,
    residual,
    output_weight,
    router,
    norm_gain,
    placed_gate_up,
    placed_down,
    routes,
    replica_pick,
    placement,
    final_gain,
):
    row_count, model_width = residual.shape
    route_count = routes.shape[1]
    experts = router.shape[1]
    place_count = placement.shape[0]
    groups = lax.axis_size("expert")
    slot_count = place_count // groups
    capacity = CAP
    projected = jnp.dot(
        head_outputs,
        lax.all_gather(output_weight, "shard", axis=0, tiled=True),
        preferred_element_type=jnp.float32,
    )
    hidden = (residual.astype(jnp.float32) + projected).astype(jnp.bfloat16)
    hidden_wide = hidden.astype(jnp.float32)
    normed = rms_scale(hidden_wide, norm_gain).astype(jnp.bfloat16)
    logits = jnp.dot(normed, router, preferred_element_type=jnp.float32)
    labels = jnp.arange(experts, dtype=jnp.int32)
    selector = (routes[..., None] == labels).astype(jnp.float32)
    chosen_logits = jnp.sum(selector * logits[:, None, :], axis=-1)
    raised = jnp.exp(chosen_logits)
    route_weight = raised / jnp.sum(raised, axis=-1, keepdims=True)
    slot_ids = choose_slots(routes, replica_pick, placement, experts).reshape(-1)
    slot_hits = (slot_ids[:, None] == jnp.arange(place_count, dtype=jnp.int32)).astype(jnp.int32)
    slot_rank = jnp.sum((jnp.cumsum(slot_hits, axis=0) - slot_hits) * slot_hits, axis=1)
    copies_out = jnp.repeat(normed, route_count, axis=0)
    gate_up, down_proj = (
        lax.all_gather(placed_gate_up, "shard", axis=1, tiled=True),
        lax.all_gather(placed_down, "shard", axis=1, tiled=True),
    )
    buffer_index = slot_ids * capacity + slot_rank
    outbound = (
        jnp.zeros((place_count * capacity, model_width), jnp.bfloat16)
        .at[buffer_index]
        .set(copies_out)
    )
    inbound = lax.all_to_all(
        outbound.reshape(groups, slot_count * capacity, model_width),
        "expert",
        split_axis=0,
        concat_axis=0,
        tiled=True,
    )
    inbound = inbound.reshape(groups, slot_count, capacity, model_width)
    answers = padded_experts(inbound, gate_up, down_proj)
    returned = lax.all_to_all(
        answers.reshape(groups, slot_count * capacity, model_width),
        "expert",
        split_axis=0,
        concat_axis=0,
        tiled=True,
    )
    returned = returned.reshape(place_count * capacity, model_width)
    gathered = returned[buffer_index].reshape(row_count, route_count, model_width)
    mixture = jnp.sum(route_weight[..., None] * gathered.astype(jnp.float32), axis=1)
    return rms_scale(hidden_wide + mixture, final_gain).astype(jnp.bfloat16)


def solution(mesh):
    by_quarters = mesh.shape["expert"] == 8 and mesh.shape["shard"] == 4
    return jax.shard_map(
        quarter_body if by_quarters else body,
        mesh=mesh,
        in_specs=(
            P(("expert", "shard"), None),
            P(("expert", "shard"), None),
            P("shard", None),
            P(),
            P(),
            P("expert", "shard", None),
            P("expert", "shard", None),
            P(("expert", "shard"), None),
            P(("expert", "shard"), None),
            P(),
            P(),
        ),
        out_specs=P(("expert", "shard"), None),
        check_vma=False,
    )
```

```python
import functools
import math

import jax
import jax.numpy as jnp
from jax import lax
from jax.experimental import pallas as pl
from jax.experimental.pallas import tpu as pltpu
from jax.sharding import PartitionSpec as P

CAP = 48


eps_norm = 1e-06
most_copies = 3


def rms_scale(values, scale_gain):
    mean_square = jnp.mean(values * values, axis=-1, keepdims=True)
    return values * lax.rsqrt(mean_square + eps_norm) * scale_gain


bf16 = jnp.bfloat16
f32 = jnp.float32
vmem_limit = 62 * 1024 * 1024
tile_rows = 512
chunks = ((0, 4), (4, 4))
any_space = pl.BlockSpec(memory_space=pl.ANY)
in_vmem = pl.BlockSpec(memory_space=pltpu.VMEM)
in_smem = pl.BlockSpec(memory_space=pltpu.SMEM)


def swap(value, axis, bits):
    size = lax.axis_size(axis)
    return lax.ppermute(value, axis, [(i, i ^ bits) for i in range(size)])


def hit_table(routes, picks, column, row, places):
    lanes = row.shape[1]
    same = column == row
    q = lax.broadcasted_iota(jnp.int32, same.shape, 0)
    p = lax.broadcasted_iota(jnp.int32, same.shape, 1) % places
    copies = jnp.sum(jnp.where(same & (q < places), 1.0, 0.0), axis=0, keepdims=True)
    rank = jnp.sum(jnp.where(same & (q < p), 1.0, 0.0), axis=0, keepdims=True)
    routes = jnp.transpose(routes.astype(f32))
    rests = [jnp.transpose(lax.rem(picks, jnp.full_like(picks, count)).astype(f32)) for count in range(2, most_copies + 1)]
    hits = jnp.zeros((routes.shape[0], lanes), f32)
    for k in range(routes.shape[1]):
        wanted = jnp.zeros(hits.shape, f32)
        for count, rest in enumerate(rests, 2):
            wanted = jnp.where(copies == count, rest[:, k:k + 1], wanted)
        hits = jnp.where((routes[:, k:k + 1] == row) & (wanted == rank), 1.0, hits)
    return hits


def quarters_kernel(weights_ref, send_ref):
    shards, _, columns = send_ref.shape
    units = columns // 2
    for q in range(shards):
        for part in range(2):
            at = (part * shards + q) * units
            send_ref[q, :, part * units:(part + 1) * units] = weights_ref[0, :, at:at + units]


def quarters(weights, first, slots, shards):
    _, depth, columns = weights.shape
    part = columns // shards
    return pl.pallas_call(
        quarters_kernel,
        out_shape=jax.ShapeDtypeStruct((shards, depth, part * slots), bf16),
        grid=(slots,),
        in_specs=[pl.BlockSpec((1, depth, columns), lambda i: (first + i, 0, 0))],
        out_specs=pl.BlockSpec((shards, depth, part), lambda i: (0, 0, i)),
        compiler_params=pltpu.CompilerParams(vmem_limit_bytes=vmem_limit),
        cost_estimate=pl.CostEstimate(flops=0, bytes_accessed=4 * depth * columns * slots, transcendentals=0),
        name="quarters",
    )(weights)


class Loads:
    def __init__(self, sems):
        self.sems = sems
        self.used = 0
        self.waiting = {}

    def start(self, name, source, target):
        copy = pltpu.make_async_copy(source, target, self.sems.at[self.used])
        copy.start()
        self.used += 1
        self.waiting.setdefault(name, []).append(copy)

    def wait(self, name):
        for copy in self.waiting.pop(name, []):
            copy.wait()


def project_kernel(
    where_ref, heads_hbm, residual_hbm, gain_hbm, router_hbm, routes_hbm, picks_hbm, experts_hbm, *refs
):
    pieces = refs[:-11]
    rows_ref, hidden_ref, weight, heads_ref, residual_ref, gain_ref, router_ref = refs[-11:-4]
    routes_ref, picks_ref, experts_ref, sems = refs[-4:]
    e = where_ref[0]
    s = where_ref[1]
    chips = len(pieces) // 2
    shards, piece, _ = pieces[0].shape
    depth = weight.shape[0] // shards
    loads = Loads(sems)
    for source, target in (
        (routes_hbm, routes_ref), (picks_hbm, picks_ref), (experts_hbm, experts_ref), (router_hbm, router_ref),
    ):
        loads.start("routing", source, target)
    for core in range(2):
        for chip in range(chips):
            for k in range(shards):
                start = pl.multiple_of((s ^ k) * depth + (e ^ (2 * chip + core)) * piece, piece)
                loads.start("weight", pieces[core * chips + chip].at[k], weight.at[pl.ds(start, piece), :])
    for source, target in ((heads_hbm, heads_ref), (residual_hbm, residual_ref), (gain_hbm, gain_ref)):
        loads.start("weight", source, target)
    loads.wait("routing")
    places = experts_ref.shape[1]
    row = experts_ref[...].astype(f32)
    row = jnp.concatenate([row, row], axis=1)
    column = jnp.transpose(jnp.broadcast_to(row, (row.shape[1], row.shape[1])))
    hits = hit_table(routes_ref[...], picks_ref[...], column, row, places)
    count = router_ref.shape[0]
    label = lax.broadcasted_iota(jnp.int32, (row.shape[1], count), 1).astype(f32)
    chosen = jnp.where(column[:, :count] == label, 1.0, 0.0).astype(bf16)
    router = jnp.dot(chosen, router_ref[...], preferred_element_type=f32).astype(bf16)
    loads.wait("weight")
    projected = jnp.dot(heads_ref[...], weight[...], preferred_element_type=f32)
    hidden = (residual_ref[...].astype(f32) + projected).astype(bf16)
    hidden_ref[...] = hidden
    normed = rms_scale(hidden.astype(f32), gain_ref[...]).astype(bf16)
    width = normed.shape[1]
    rows_ref[:, :width] = normed
    logits = lax.dot_general(normed, router, (((1,), (1,)), ((), ())), preferred_element_type=f32)
    raised = jnp.where(hits > 0, jnp.exp(logits), 0.0)
    total = jnp.sum(raised, axis=-1, keepdims=True) * 0.5
    share = raised / total
    high = share.astype(bf16)
    low = (share - high.astype(f32)).astype(bf16)
    lane = lax.broadcasted_iota(jnp.int32, share.shape, 1)
    rows_ref[:, width:] = jnp.where(lane < places, high.astype(f32), low.astype(f32)).astype(bf16)


def project(where, heads, residual, gain, router, routes, picks, placement, pieces):
    rows, width = residual.shape
    pairs = 2 * placement.shape[0]
    places = placement.shape[0]
    operands = (
        heads, residual, gain.reshape(1, -1), router.T, routes.T, picks.T, placement.reshape(1, -1), *pieces,
    )
    count = len(operands) + len(pieces) * (pieces[0].shape[0] - 1)
    return pl.pallas_call(
        project_kernel,
        out_shape=(
            jax.ShapeDtypeStruct((rows, width + pairs), bf16),
            jax.ShapeDtypeStruct((rows, width), bf16),
        ),
        in_specs=[in_smem] + [any_space] * len(operands),
        out_specs=(in_vmem, in_vmem),
        scratch_shapes=[
            pltpu.VMEM((width, width), bf16),
            pltpu.VMEM((rows, width), bf16),
            pltpu.VMEM((rows, width), bf16),
            pltpu.VMEM((1, width), f32),
            pltpu.VMEM(router.shape[::-1], bf16),
            pltpu.VMEM(routes.shape[::-1], jnp.int32),
            pltpu.VMEM(picks.shape[::-1], jnp.int32),
            pltpu.VMEM((1, places), jnp.int32),
            pltpu.SemaphoreType.DMA((count,)),
        ],
        compiler_params=pltpu.CompilerParams(vmem_limit_bytes=vmem_limit),
        cost_estimate=pl.CostEstimate(
            flops=2 * rows * width * width, bytes_accessed=3 * width * width, transcendentals=rows * pairs
        ),
        name="project",
    )(where, *operands)


def activate(both, shares, first, slots):
    units = shares.shape[1]
    pairs = shares.shape[1]
    place = lax.broadcasted_iota(jnp.int32, (pairs, slots * units), 0) % (pairs // 2)
    lane = lax.broadcasted_iota(jnp.int32, (pairs, slots * units), 1) // units
    spread = jnp.where(place == lane + first, 1.0, 0.0).astype(bf16)
    factor = jnp.dot(shares, spread, preferred_element_type=f32)
    parts = []
    for slot in range(slots):
        gate = both[:, 2 * slot * units:(2 * slot + 1) * units]
        up = both[:, (2 * slot + 1) * units:(2 * slot + 2) * units]
        act = gate / (1.0 + jnp.exp(-gate)) * up
        parts.append((act * factor[:, slot * units:(slot + 1) * units]).astype(bf16))
    return parts


def slots_kernel(slot_sets, group_slots, block_count, has_sums, cut, where_ref, *refs):
    refs = list(refs)

    def take(count):
        taken, refs[:] = refs[:count], refs[count:]
        return taken

    blocks = take(block_count)
    sources = take(len(slot_sets))
    downs = take(2)
    earlier = take(1)[0] if has_sums else None
    outs = take(4 if cut else 1)
    sets = len(slot_sets)
    weights = take(sets)
    x, total, act, down, weight_sems, x_sems, sum_sems, out_sems = refs
    tiles, tile_rows, _ = x.shape
    width = weights[0].shape[0]
    units = x.shape[2] - width

    def load_weights(i):
        shards, depth, _ = sources[i].shape
        for q in range(shards):
            target = weights[i].at[pl.ds(q * depth, depth), :]
            pltpu.make_async_copy(sources[i].at[q], target, weight_sems.at[i]).start()

    def load_tile(tile):
        at = 0
        for block in blocks:
            rows = block.shape[0]
            if at // tile_rows == tile:
                target = x.at[tile, pl.ds(at % tile_rows, rows), :]
                pltpu.make_async_copy(block, target, x_sems.at[tile]).start()
            at += rows

    load_weights(0)
    for tile in range(tiles):
        load_tile(tile)
    for i in range(1, sets):
        load_weights(i)
    at = 0
    for flip, first, count in slot_sets:
        source, target = downs[flip].at[pl.ds(first * units, count * units), :], down.at[pl.ds(at, count * units), :]
        pltpu.make_async_copy(source, target, weight_sems.at[sets]).start()
        at += count * units
    for tile in range(tiles):
        if has_sums:
            source = earlier.at[pl.ds(tile * tile_rows, tile_rows), :]
            pltpu.make_async_copy(source, total.at[tile], sum_sems.at[tile]).start()

    at = 0
    for i, (flip, first, count) in enumerate(slot_sets):
        pltpu.make_async_copy(weights[i], weights[i], weight_sems.at[i]).wait()
        place = (where_ref[0] ^ flip) * group_slots + first

        @pl.loop(0, tiles)
        def _(tile, i=i, at=at, count=count, place=place):
            if i == 0:
                pltpu.make_async_copy(x.at[tile], x.at[tile], x_sems.at[tile]).wait()
            both = jnp.dot(x[tile, :, :width], weights[i][...], preferred_element_type=f32)
            parts = activate(both, x[tile, :, width:], place, count)
            act[tile, :, at:at + count * units] = jnp.concatenate(parts, axis=1)

        at += count * units
    pltpu.make_async_copy(down, down, weight_sems.at[sets]).wait()

    @pl.loop(0, tiles)
    def _(tile):
        added = jnp.dot(act[tile], down[...], preferred_element_type=f32)
        if has_sums:
            pltpu.make_async_copy(total.at[tile], total.at[tile], sum_sems.at[tile]).wait()
            added = added + total[tile].astype(f32)
        total[tile] = added.astype(bf16)
        if not cut:
            target = outs[0].at[pl.ds(tile * tile_rows, tile_rows), :]
            pltpu.make_async_copy(total.at[tile], target, out_sems.at[tile]).start()

    if cut:
        rows, half = blocks[0].shape[0], width // 2
        parts = block_count // 4
        copies = []
        for part in range(parts):
            place = part if cut == "ordered" else part ^ (1 - where_ref[2])
            for out, chips, column in zip(outs, ((1, 3), (2, 3), (0, 2), (0, 1)), (0, half, 0, half)):
                for i, chip in enumerate(chips):
                    tile, at = divmod((4 * part + chip) * rows, tile_rows)
                    source = total.at[tile, pl.ds(at, rows), pl.ds(column, half)]
                    target = out.at[i, place]
                    copies.append(pltpu.make_async_copy(source, target, out_sems.at[len(copies)]))
        for copy in copies:
            copy.start()
        for copy in copies:
            copy.wait()
    else:
        @pl.loop(0, tiles)
        def _(tile):
            target = outs[0].at[pl.ds(tile * tile_rows, tile_rows), :]
            pltpu.make_async_copy(total.at[tile], target, out_sems.at[tile]).wait()


def slots_block(where, blocks, sources, slot_sets, downs, earlier, group_slots, cut=None):
    rows = sum(block.shape[0] for block in blocks)
    wide = blocks[0].shape[1]
    shards, depth, _ = sources[0].shape
    width = downs[0].shape[1]
    columns = sum(source.shape[2] for source in sources)
    tiles = rows // tile_rows
    if cut:
        out_shape = [jax.ShapeDtypeStruct((2, len(blocks) // 4, blocks[0].shape[0], width // 2), bf16)] * 4
    else:
        out_shape = [jax.ShapeDtypeStruct((rows, width), bf16)]
    return pl.pallas_call(
        functools.partial(slots_kernel, slot_sets, group_slots, len(blocks), bool(earlier), cut),
        out_shape=out_shape,
        in_specs=[in_smem] + [any_space] * (len(blocks) + len(sources) + 2 + len(earlier)),
        out_specs=[any_space] * len(out_shape),
        scratch_shapes=[pltpu.VMEM((depth * shards, source.shape[2]), bf16) for source in sources]
        + [
            pltpu.VMEM((tiles, tile_rows, wide), bf16),
            pltpu.VMEM((tiles, tile_rows, width), bf16),
            pltpu.VMEM((tiles, tile_rows, columns // 2), bf16),
            pltpu.VMEM((columns // 2, width), bf16),
            pltpu.SemaphoreType.DMA((len(sources) + 1,)),
            pltpu.SemaphoreType.DMA((tiles,)),
            pltpu.SemaphoreType.DMA((tiles,)),
            pltpu.SemaphoreType.DMA((max(tiles, 2 * len(blocks)),)),
        ],
        compiler_params=pltpu.CompilerParams(vmem_limit_bytes=vmem_limit),
        cost_estimate=pl.CostEstimate(
            flops=2 * rows * columns * (depth * shards + width // 2),
            bytes_accessed=2 * (rows * (wide + 2 * width) + columns * (depth * shards + width // 2)),
            transcendentals=rows * columns // 2,
        ),
        name="slots_block",
    )(where, *blocks, *sources, *downs, *earlier)


def after(value, *events):
    return lax.optimization_barrier((value, *events))[0]


def chip_gather(block):
    return [block] + [swap(block, "expert", bits) for bits in (2, 4, 6)]


def core_gather(chips):
    return chips + [swap(chip, "expert", 1) for chip in chips]


def stage(*values):
    return lax.optimization_barrier(values)


def add(left, right):
    return (left.astype(f32) + right.astype(f32)).astype(bf16)


def quarter_body(
    head_outputs,
    residual,
    output_weight,
    router,
    norm_gain,
    placed_gate_up,
    placed_down,
    routes,
    replica_pick,
    placement,
    final_gain,
):
    rows, width = residual.shape
    slots, depth, columns = placed_gate_up.shape
    devices, shards = lax.axis_size("expert"), lax.axis_size("shard")
    e, s = lax.axis_index("expert"), lax.axis_index("shard")
    inner = (s == 1) | (s == 2)
    where = jnp.stack([e, s, inner]).astype(jnp.int32)
    hidden_units = columns // 2
    units = hidden_units // shards

    piece = output_weight.shape[0] // devices
    own = lax.dynamic_slice_in_dim(output_weight, e * piece, piece, 0)
    over_z = jnp.stack([own] + [swap(own, "shard", k) for k in range(1, shards)])

    sends = [quarters(placed_gate_up, first, count, shards) for first, count in chunks]

    def exchange(send):
        return lax.all_to_all(send, "shard", split_axis=0, concat_axis=0, tiled=True)

    over_z, send = stage(over_z, sends[0])
    weights = [exchange(send)]
    pieces = core_gather(chip_gather(over_z))
    block, hidden = project(where, head_outputs, residual, norm_gain, router, routes, replica_pick, placement, pieces)

    cross = [(1, 2), (2, 1)]
    outward = [(1, 0), (2, 3)]

    own_chips = chip_gather(block)
    near = swap(block, "shard", 1)
    first_in = lax.ppermute(block, "shard", cross)
    second_in = lax.ppermute(near, "shard", cross)
    near, first_in, second_in, send, *own_chips = stage(near, first_in, second_in, sends[1], *own_chips)

    near_chips = chip_gather(near)
    first_out = lax.ppermute(first_in, "shard", outward)
    second_out = lax.ppermute(second_in, "shard", outward)
    first_out, second_out, weights[0], *near_chips = stage(first_out, second_out, weights[0], *near_chips)

    weights.append(exchange(after(send, weights[0])))
    far_a = jnp.where(inner, first_in, first_out)
    far_a_chips = chip_gather(far_a)

    down = placed_down.reshape(slots * units, width)
    downs = [down, swap(after(down, near), "expert", 1)]
    others = [swap(weights[0], "expert", 1)]
    def run(blocks, which, earlier, cut=None):
        sources, sets = [], []
        for chunk in range(len(chunks))[which]:
            sources += [weights[chunk], others[chunk]]
            sets += [(0, *chunks[chunk]), (1, *chunks[chunk])]
        return slots_block(where, blocks, sources, tuple(sets), downs, earlier, slots, cut)

    (early,) = run(near_chips + own_chips, slice(0, 1), [])
    early, *far_a_chips = stage(early, *far_a_chips)

    far_b = jnp.where(inner, second_in, second_out)
    far_b_chips = chip_gather(far_b)
    far_b_chips = stage(*far_b_chips)
    (late,) = run(list(far_a_chips) + list(far_b_chips), slice(0, 1), [])
    weights[1], late = stage(weights[1], late)
    others.append(swap(weights[1], "expert", 1))

    sums = {}
    far = run(list(far_a_chips) + list(far_b_chips), slice(1, 2), [late], "labelled")
    far_x, far_y = swap(far[0], "expert", 2), swap(far[1], "expert", 4)
    close = run(near_chips + own_chips, slice(1, 2), [after(early, far[2])], "ordered")
    far_x, far_y, *close = stage(far_x, far_y, *close)
    close_x, close_y = swap(close[0], "expert", 2), swap(close[1], "expert", 4)
    for pair, left, right, a_x, b_y in (
        ((3, 2), far[2], far[3], far_x, far_y), ((1, 0), close[2], close[3], close_x, close_y)
    ):
        a_y = swap(add(left[1], a_x[1]), "expert", 4)
        b_x = swap(add(right[1], b_y[1]), "expert", 2)
        left = left[0].astype(f32) + a_x[0].astype(f32) + a_y.astype(f32)
        right = right[0].astype(f32) + b_y[0].astype(f32) + b_x.astype(f32)
        for i, k in enumerate(pair):
            sums[k] = jnp.concatenate([left[i], right[i]], axis=1)
    sent = [swap(sums[k].astype(bf16), "shard", k) for k in range(1, shards)]
    total = hidden.astype(f32) + sums[0]
    for part in sent:
        total = total + part.astype(f32)
    return rms_scale(total, final_gain).astype(bf16)


def choose_slots(routes, replica_pick, placement, experts):
    labels = jnp.arange(experts, dtype=jnp.int32)
    holder_mask = (placement[None, :] == labels[:, None]).astype(jnp.int32)
    before = jnp.cumsum(holder_mask, axis=1) - holder_mask
    copies = jnp.sum(holder_mask, axis=1)
    places = jnp.arange(placement.shape[0], dtype=jnp.int32)
    route_hits = (routes[..., None] == labels).astype(jnp.int32)
    held_count = jnp.sum(route_hits * copies, axis=-1)
    wanted = replica_pick % held_count
    chosen = jnp.zeros(routes.shape, jnp.int32)
    for replica in range(most_copies):
        column = jnp.sum(
            holder_mask * (before == replica).astype(jnp.int32) * places[None, :], axis=1
        )
        candidate = jnp.sum(route_hits * column, axis=-1)
        chosen = jnp.where(wanted == replica, candidate, chosen)
    return chosen


def padded_experts(inbound, gate_up, down_proj):
    sources, slot_count, slot_depth, model_width = inbound.shape
    per_source = slot_count * slot_depth
    upper_bound = max(1, 1024 // per_source)
    power_two = 1 << upper_bound.bit_length() - 1
    group_size = math.gcd(sources, power_two)
    stacked = inbound.reshape(
        sources // group_size, group_size, slot_count, slot_depth, model_width
    )
    hidden_units = down_proj.shape[1]

    def apply_block(block_part):
        both_parts = jnp.einsum(
            "bjmd,jdf->bjmf", block_part, gate_up, preferred_element_type=jnp.float32
        )
        activated = (
            jax.nn.silu(both_parts[..., :hidden_units]) * both_parts[..., hidden_units:]
        ).astype(jnp.bfloat16)
        return jnp.einsum(
            "bjmf,jfd->bjmd", activated, down_proj, preferred_element_type=jnp.float32
        ).astype(jnp.bfloat16)

    return lax.map(apply_block, stacked).reshape(inbound.shape)


def body(
    head_outputs,
    residual,
    output_weight,
    router,
    norm_gain,
    placed_gate_up,
    placed_down,
    routes,
    replica_pick,
    placement,
    final_gain,
):
    row_count, model_width = residual.shape
    route_count = routes.shape[1]
    experts = router.shape[1]
    place_count = placement.shape[0]
    groups = lax.axis_size("expert")
    slot_count = place_count // groups
    capacity = CAP
    projected = jnp.dot(
        head_outputs,
        lax.all_gather(output_weight, "shard", axis=0, tiled=True),
        preferred_element_type=jnp.float32,
    )
    hidden = (residual.astype(jnp.float32) + projected).astype(jnp.bfloat16)
    hidden_wide = hidden.astype(jnp.float32)
    normed = rms_scale(hidden_wide, norm_gain).astype(jnp.bfloat16)
    logits = jnp.dot(normed, router, preferred_element_type=jnp.float32)
    labels = jnp.arange(experts, dtype=jnp.int32)
    selector = (routes[..., None] == labels).astype(jnp.float32)
    chosen_logits = jnp.sum(selector * logits[:, None, :], axis=-1)
    raised = jnp.exp(chosen_logits)
    route_weight = raised / jnp.sum(raised, axis=-1, keepdims=True)
    slot_ids = choose_slots(routes, replica_pick, placement, experts).reshape(-1)
    slot_hits = (slot_ids[:, None] == jnp.arange(place_count, dtype=jnp.int32)).astype(jnp.int32)
    slot_rank = jnp.sum((jnp.cumsum(slot_hits, axis=0) - slot_hits) * slot_hits, axis=1)
    copies_out = jnp.repeat(normed, route_count, axis=0)
    gate_up, down_proj = (
        lax.all_gather(placed_gate_up, "shard", axis=1, tiled=True),
        lax.all_gather(placed_down, "shard", axis=1, tiled=True),
    )
    buffer_index = slot_ids * capacity + slot_rank
    outbound = (
        jnp.zeros((place_count * capacity, model_width), jnp.bfloat16)
        .at[buffer_index]
        .set(copies_out)
    )
    inbound = lax.all_to_all(
        outbound.reshape(groups, slot_count * capacity, model_width),
        "expert",
        split_axis=0,
        concat_axis=0,
        tiled=True,
    )
    inbound = inbound.reshape(groups, slot_count, capacity, model_width)
    answers = padded_experts(inbound, gate_up, down_proj)
    returned = lax.all_to_all(
        answers.reshape(groups, slot_count * capacity, model_width),
        "expert",
        split_axis=0,
        concat_axis=0,
        tiled=True,
    )
    returned = returned.reshape(place_count * capacity, model_width)
    gathered = returned[buffer_index].reshape(row_count, route_count, model_width)
    mixture = jnp.sum(route_weight[..., None] * gathered.astype(jnp.float32), axis=1)
    return rms_scale(hidden_wide + mixture, final_gain).astype(jnp.bfloat16)


def solution(mesh):
    by_quarters = mesh.shape["expert"] == 8 and mesh.shape["shard"] == 4
    return jax.shard_map(
        quarter_body if by_quarters else body,
        mesh=mesh,
        in_specs=(
            P(("expert", "shard"), None),
            P(("expert", "shard"), None),
            P("shard", None),
            P(),
            P(),
            P("expert", "shard", None),
            P("expert", "shard", None),
            P(("expert", "shard"), None),
            P(("expert", "shard"), None),
            P(),
            P(),
        ),
        out_specs=P(("expert", "shard"), None),
        check_vma=False,
    )
```

```python
import functools
import math

import jax
import jax.numpy as jnp
from jax import lax
from jax.experimental import pallas as pl
from jax.experimental.pallas import tpu as pltpu
from jax.sharding import PartitionSpec as P

CAP = 48


eps_norm = 1e-06
most_copies = 3


def rms_scale(values, scale_gain):
    mean_square = jnp.mean(values * values, axis=-1, keepdims=True)
    return values * lax.rsqrt(mean_square + eps_norm) * scale_gain


bf16 = jnp.bfloat16
f32 = jnp.float32
vmem_limit = 62 * 1024 * 1024
tile_rows = 512
chunks = ((0, 3), (3, 5))
any_space = pl.BlockSpec(memory_space=pl.ANY)
in_vmem = pl.BlockSpec(memory_space=pltpu.VMEM)
in_smem = pl.BlockSpec(memory_space=pltpu.SMEM)


def swap(value, axis, bits):
    size = lax.axis_size(axis)
    return lax.ppermute(value, axis, [(i, i ^ bits) for i in range(size)])


def hit_table(routes, picks, column, row, places):
    lanes = row.shape[1]
    same = column == row
    q = lax.broadcasted_iota(jnp.int32, same.shape, 0)
    p = lax.broadcasted_iota(jnp.int32, same.shape, 1) % places
    copies = jnp.sum(jnp.where(same & (q < places), 1.0, 0.0), axis=0, keepdims=True)
    rank = jnp.sum(jnp.where(same & (q < p), 1.0, 0.0), axis=0, keepdims=True)
    routes = jnp.transpose(routes.astype(f32))
    rests = [jnp.transpose(lax.rem(picks, jnp.full_like(picks, count)).astype(f32)) for count in range(2, most_copies + 1)]
    hits = jnp.zeros((routes.shape[0], lanes), f32)
    for k in range(routes.shape[1]):
        wanted = jnp.zeros(hits.shape, f32)
        for count, rest in enumerate(rests, 2):
            wanted = jnp.where(copies == count, rest[:, k:k + 1], wanted)
        hits = jnp.where((routes[:, k:k + 1] == row) & (wanted == rank), 1.0, hits)
    return hits


def quarters_kernel(weights_ref, send_ref):
    shards, _, columns = send_ref.shape
    units = columns // 2
    for q in range(shards):
        for part in range(2):
            at = (part * shards + q) * units
            send_ref[q, :, part * units:(part + 1) * units] = weights_ref[0, :, at:at + units]


def quarters(weights, first, slots, shards):
    _, depth, columns = weights.shape
    part = columns // shards
    return pl.pallas_call(
        quarters_kernel,
        out_shape=jax.ShapeDtypeStruct((shards, depth, part * slots), bf16),
        grid=(slots,),
        in_specs=[pl.BlockSpec((1, depth, columns), lambda i: (first + i, 0, 0))],
        out_specs=pl.BlockSpec((shards, depth, part), lambda i: (0, 0, i)),
        compiler_params=pltpu.CompilerParams(vmem_limit_bytes=vmem_limit),
        cost_estimate=pl.CostEstimate(flops=0, bytes_accessed=4 * depth * columns * slots, transcendentals=0),
        name="quarters",
    )(weights)


class Loads:
    def __init__(self, sems):
        self.sems = sems
        self.used = 0
        self.waiting = {}

    def start(self, name, source, target):
        copy = pltpu.make_async_copy(source, target, self.sems.at[self.used])
        copy.start()
        self.used += 1
        self.waiting.setdefault(name, []).append(copy)

    def wait(self, name):
        for copy in self.waiting.pop(name, []):
            copy.wait()


def project_kernel(
    where_ref, heads_hbm, residual_hbm, gain_hbm, router_hbm, routes_hbm, picks_hbm, experts_hbm, *refs
):
    pieces = refs[:-11]
    rows_ref, hidden_ref, weight, heads_ref, residual_ref, gain_ref, router_ref = refs[-11:-4]
    routes_ref, picks_ref, experts_ref, sems = refs[-4:]
    e = where_ref[0]
    s = where_ref[1]
    chips = len(pieces) // 2
    shards, piece, _ = pieces[0].shape
    depth = weight.shape[0] // shards
    loads = Loads(sems)
    for source, target in (
        (routes_hbm, routes_ref), (picks_hbm, picks_ref), (experts_hbm, experts_ref), (router_hbm, router_ref),
    ):
        loads.start("routing", source, target)
    for core in range(2):
        for chip in range(chips):
            for k in range(shards):
                start = pl.multiple_of((s ^ k) * depth + (e ^ (2 * chip + core)) * piece, piece)
                loads.start("weight", pieces[core * chips + chip].at[k], weight.at[pl.ds(start, piece), :])
    for source, target in ((heads_hbm, heads_ref), (residual_hbm, residual_ref), (gain_hbm, gain_ref)):
        loads.start("weight", source, target)
    loads.wait("routing")
    places = experts_ref.shape[1]
    row = experts_ref[...].astype(f32)
    row = jnp.concatenate([row, row], axis=1)
    column = jnp.transpose(jnp.broadcast_to(row, (row.shape[1], row.shape[1])))
    hits = hit_table(routes_ref[...], picks_ref[...], column, row, places)
    count = router_ref.shape[0]
    label = lax.broadcasted_iota(jnp.int32, (row.shape[1], count), 1).astype(f32)
    chosen = jnp.where(column[:, :count] == label, 1.0, 0.0).astype(bf16)
    router = jnp.dot(chosen, router_ref[...], preferred_element_type=f32).astype(bf16)
    loads.wait("weight")
    projected = jnp.dot(heads_ref[...], weight[...], preferred_element_type=f32)
    hidden = (residual_ref[...].astype(f32) + projected).astype(bf16)
    hidden_ref[...] = hidden
    normed = rms_scale(hidden.astype(f32), gain_ref[...]).astype(bf16)
    width = normed.shape[1]
    rows_ref[:, :width] = normed
    logits = lax.dot_general(normed, router, (((1,), (1,)), ((), ())), preferred_element_type=f32)
    raised = jnp.where(hits > 0, jnp.exp(logits), 0.0)
    total = jnp.sum(raised, axis=-1, keepdims=True) * 0.5
    share = raised / total
    high = share.astype(bf16)
    low = (share - high.astype(f32)).astype(bf16)
    lane = lax.broadcasted_iota(jnp.int32, share.shape, 1)
    rows_ref[:, width:] = jnp.where(lane < places, high.astype(f32), low.astype(f32)).astype(bf16)


def project(where, heads, residual, gain, router, routes, picks, placement, pieces):
    rows, width = residual.shape
    pairs = 2 * placement.shape[0]
    places = placement.shape[0]
    operands = (
        heads, residual, gain.reshape(1, -1), router.T, routes.T, picks.T, placement.reshape(1, -1), *pieces,
    )
    count = len(operands) + len(pieces) * (pieces[0].shape[0] - 1)
    return pl.pallas_call(
        project_kernel,
        out_shape=(
            jax.ShapeDtypeStruct((rows, width + pairs), bf16),
            jax.ShapeDtypeStruct((rows, width), bf16),
        ),
        in_specs=[in_smem] + [any_space] * len(operands),
        out_specs=(in_vmem, in_vmem),
        scratch_shapes=[
            pltpu.VMEM((width, width), bf16),
            pltpu.VMEM((rows, width), bf16),
            pltpu.VMEM((rows, width), bf16),
            pltpu.VMEM((1, width), f32),
            pltpu.VMEM(router.shape[::-1], bf16),
            pltpu.VMEM(routes.shape[::-1], jnp.int32),
            pltpu.VMEM(picks.shape[::-1], jnp.int32),
            pltpu.VMEM((1, places), jnp.int32),
            pltpu.SemaphoreType.DMA((count,)),
        ],
        compiler_params=pltpu.CompilerParams(vmem_limit_bytes=vmem_limit),
        cost_estimate=pl.CostEstimate(
            flops=2 * rows * width * width, bytes_accessed=3 * width * width, transcendentals=rows * pairs
        ),
        name="project",
    )(where, *operands)


def activate(both, shares, first, slots):
    units = shares.shape[1]
    pairs = shares.shape[1]
    place = lax.broadcasted_iota(jnp.int32, (pairs, slots * units), 0) % (pairs // 2)
    lane = lax.broadcasted_iota(jnp.int32, (pairs, slots * units), 1) // units
    spread = jnp.where(place == lane + first, 1.0, 0.0).astype(bf16)
    factor = jnp.dot(shares, spread, preferred_element_type=f32)
    parts = []
    for slot in range(slots):
        gate = both[:, 2 * slot * units:(2 * slot + 1) * units]
        up = both[:, (2 * slot + 1) * units:(2 * slot + 2) * units]
        act = gate / (1.0 + jnp.exp(-gate)) * up
        parts.append((act * factor[:, slot * units:(slot + 1) * units]).astype(bf16))
    return parts


def slots_kernel(slot_sets, group_slots, block_rows, source_counts, sum_rows, cut, where_ref, *refs):
    refs = list(refs)

    def take(count):
        taken, refs[:] = refs[:count], refs[count:]
        return taken

    block_count, has_sums = len(block_rows), bool(sum_rows)
    blocks = take(block_count)
    sources = [take(count) for count in source_counts]
    downs = take(2)
    earlier = take(len(sum_rows))
    outs = take(4 if cut else 1)
    sets = len(slot_sets)
    weights = take(sets)
    x, total, act, down, weight_sems, x_sems, sum_sems, out_sems = refs
    tiles, tile_rows, _ = x.shape
    width = weights[0].shape[0]
    units = x.shape[2] - width

    def load_weights(i):
        if len(sources[i]) == 1:
            blocks = [sources[i][0].at[q] for q in range(sources[i][0].shape[0])]
        else:
            blocks = sources[i]
        for k, block in enumerate(blocks):
            depth = block.shape[0]
            q = k if len(sources[i]) == 1 else where_ref[1] ^ k
            target = weights[i].at[pl.ds(pl.multiple_of(q * depth, depth), depth), :]
            pltpu.make_async_copy(block, target, weight_sems.at[i]).start()

    def load_tile(tile):
        rows = tiles * tile_rows // block_count
        for i, (block, first) in enumerate(zip(blocks, block_rows)):
            if i * rows // tile_rows == tile:
                target = x.at[tile, pl.ds(i * rows % tile_rows, rows), :]
                pltpu.make_async_copy(block.at[pl.ds(first, rows), :], target, x_sems.at[tile]).start()

    load_weights(0)
    for tile in range(tiles):
        load_tile(tile)
    for i in range(1, sets):
        load_weights(i)
    at = 0
    for flip, first, count in slot_sets:
        source, target = downs[flip].at[pl.ds(first * units, count * units), :], down.at[pl.ds(at, count * units), :]
        pltpu.make_async_copy(source, target, weight_sems.at[sets]).start()
        at += count * units
    for tile in range(tiles):
        if has_sums:
            source = earlier[tile].at[pl.ds(sum_rows[tile], tile_rows), :]
            pltpu.make_async_copy(source, total.at[tile], sum_sems.at[tile]).start()

    at = 0
    for i, (flip, first, count) in enumerate(slot_sets):
        pltpu.make_async_copy(weights[i], weights[i], weight_sems.at[i]).wait()
        place = (where_ref[0] ^ flip) * group_slots + first

        @pl.loop(0, tiles)
        def _(tile, i=i, at=at, count=count, place=place):
            if i == 0:
                pltpu.make_async_copy(x.at[tile], x.at[tile], x_sems.at[tile]).wait()
            both = jnp.dot(x[tile, :, :width], weights[i][...], preferred_element_type=f32)
            parts = activate(both, x[tile, :, width:], place, count)
            act[tile, :, at:at + count * units] = jnp.concatenate(parts, axis=1)

        at += count * units
    pltpu.make_async_copy(down, down, weight_sems.at[sets]).wait()

    @pl.loop(0, tiles)
    def _(tile):
        added = jnp.dot(act[tile], down[...], preferred_element_type=f32)
        if has_sums:
            pltpu.make_async_copy(total.at[tile], total.at[tile], sum_sems.at[tile]).wait()
            added = added + total[tile].astype(f32)
        total[tile] = added.astype(bf16)
        if not cut:
            target = outs[0].at[pl.ds(tile * tile_rows, tile_rows), :]
            pltpu.make_async_copy(total.at[tile], target, out_sems.at[tile]).start()

    if cut:
        rows, half = tiles * tile_rows // block_count, width // 2
        parts = block_count // 4
        copies = []
        for part in range(parts):
            place = part if cut == "ordered" else part ^ (1 - where_ref[2])
            for out, chips, column in zip(outs, ((1, 3), (2, 3), (0, 2), (0, 1)), (0, half, 0, half)):
                for i, chip in enumerate(chips):
                    tile, at = divmod((4 * part + chip) * rows, tile_rows)
                    source = total.at[tile, pl.ds(at, rows), pl.ds(column, half)]
                    target = out.at[i, place]
                    copies.append(pltpu.make_async_copy(source, target, out_sems.at[len(copies)]))
        for copy in copies:
            copy.start()
        for copy in copies:
            copy.wait()
    else:
        @pl.loop(0, tiles)
        def _(tile):
            target = outs[0].at[pl.ds(tile * tile_rows, tile_rows), :]
            pltpu.make_async_copy(total.at[tile], target, out_sems.at[tile]).wait()


def slots_block(where, tokens, blocks, sources, slot_sets, downs, earlier, group_slots, cut=None):
    block_rows = tuple(first for _, first in blocks)
    sum_rows = tuple(first for _, first in earlier)
    blocks, earlier = [block for block, _ in blocks], [total for total, _ in earlier]
    rows, wide = len(blocks) * tokens, blocks[0].shape[1]
    width = downs[0].shape[1]
    wides = [source[0].shape[-1] for source in sources]
    columns = sum(wides)
    source_counts = tuple(len(source) for source in sources)
    sources = [block for source in sources for block in source]
    tiles = rows // tile_rows
    if cut:
        out_shape = [jax.ShapeDtypeStruct((2, len(blocks) // 4, tokens, width // 2), bf16)] * 4
    else:
        out_shape = [jax.ShapeDtypeStruct((rows, width), bf16)]
    return pl.pallas_call(
        functools.partial(slots_kernel, slot_sets, group_slots, block_rows, source_counts, sum_rows, cut),
        out_shape=out_shape,
        in_specs=[in_smem] + [any_space] * (len(blocks) + len(sources) + 2 + len(earlier)),
        out_specs=[any_space] * len(out_shape),
        scratch_shapes=[pltpu.VMEM((width, columns), bf16) for columns in wides]
        + [
            pltpu.VMEM((tiles, tile_rows, wide), bf16),
            pltpu.VMEM((tiles, tile_rows, width), bf16),
            pltpu.VMEM((tiles, tile_rows, columns // 2), bf16),
            pltpu.VMEM((columns // 2, width), bf16),
            pltpu.SemaphoreType.DMA((len(wides) + 1,)),
            pltpu.SemaphoreType.DMA((tiles,)),
            pltpu.SemaphoreType.DMA((tiles,)),
            pltpu.SemaphoreType.DMA((max(tiles, 2 * len(blocks)),)),
        ],
        compiler_params=pltpu.CompilerParams(vmem_limit_bytes=vmem_limit),
        cost_estimate=pl.CostEstimate(
            flops=3 * rows * columns * width,
            bytes_accessed=2 * rows * (wide + 2 * width) + 3 * columns * width,
            transcendentals=rows * columns // 2,
        ),
        name="slots_block",
    )(where, *blocks, *sources, *downs, *earlier)


def after(value, *events):
    return lax.optimization_barrier((value, *events))[0]


def chip_gather(block):
    return [block] + [swap(block, "expert", bits) for bits in (2, 4, 6)]


def core_gather(chips):
    return chips + [swap(chip, "expert", 1) for chip in chips]


def stage(*values):
    return lax.optimization_barrier(values)


def add(left, right):
    return (left.astype(f32) + right.astype(f32)).astype(bf16)


def quarter_body(
    head_outputs,
    residual,
    output_weight,
    router,
    norm_gain,
    placed_gate_up,
    placed_down,
    routes,
    replica_pick,
    placement,
    final_gain,
):
    rows, width = residual.shape
    slots, depth, columns = placed_gate_up.shape
    devices, shards = lax.axis_size("expert"), lax.axis_size("shard")
    e, s = lax.axis_index("expert"), lax.axis_index("shard")
    inner = (s == 1) | (s == 2)
    where = jnp.stack([e, s, inner]).astype(jnp.int32)
    hidden_units = columns // 2
    units = hidden_units // shards

    piece = output_weight.shape[0] // devices
    own = lax.dynamic_slice_in_dim(output_weight, e * piece, piece, 0)
    over_z = jnp.stack([own] + [swap(own, "shard", k) for k in range(1, shards)])

    sends = [quarters(placed_gate_up, *chunks[0], shards)]

    def exchange(send):
        return lax.all_to_all(send, "shard", split_axis=0, concat_axis=0, tiled=True)

    over_z, send = stage(over_z, sends[0])
    weights = [exchange(send)]
    down = placed_down.reshape(slots * units, width)
    pieces = chip_gather(over_z)
    sends.append(quarters(after(placed_gate_up, pieces[1]), *chunks[1], shards))
    *pieces, other_down, sends[1] = stage(*pieces, swap(after(down, over_z), "expert", 1), sends[1])
    pieces = core_gather(pieces)
    downs = [down, other_down]
    block, hidden = project(where, head_outputs, residual, norm_gain, router, routes, replica_pick, placement, pieces)

    cross = [(1, 2), (2, 1)]
    outward = [(1, 0), (2, 3)]

    own_chips = chip_gather(block)
    near = swap(block, "shard", 1)
    first_in = lax.ppermute(block, "shard", cross)
    second_in = lax.ppermute(near, "shard", cross)
    parts = [lax.dynamic_index_in_dim(sends[1], s ^ k, 0, keepdims=False) for k in range(shards)]
    near, first_in, second_in, *rest = stage(near, first_in, second_in, *parts, *own_chips)
    parts, own_chips = rest[:4], rest[4:]

    near_chips = [near, swap(near, "expert", 2), swap(near, "expert", 4)]
    first_out = lax.ppermute(first_in, "shard", outward)
    second_out = lax.ppermute(second_in, "shard", outward)
    part_in = lax.ppermute(parts[3], "shard", cross)
    first_out, second_out, weights[0], part_in, *rest = stage(
        first_out, second_out, weights[0], part_in, *parts, *near_chips
    )
    parts, near_chips = list(rest[:4]), list(rest[4:])

    parts[1] = swap(parts[1], "shard", 1)
    parts[2] = swap(parts[2], "shard", 2)
    far = jnp.concatenate([jnp.where(inner, first_in, first_out), jnp.where(inner, second_in, second_out)])
    far_chips = chip_gather(far)

    weights = [[weights[0]]]
    others = [[swap(weights[0][0], "expert", 1)]]
    def run(blocks, which, earlier, cut=None):
        sources, sets = [], []
        for chunk in range(len(chunks))[which]:
            sources += [weights[chunk], others[chunk]]
            sets += [(0, *chunks[chunk]), (1, *chunks[chunk])]
        return slots_block(where, rows, blocks, sources, tuple(sets), downs, earlier, slots, cut)

    own_blocks = [(chip, 0) for chip in own_chips]
    (early,) = run(own_blocks, slice(0, 1), [])
    early, *rest = stage(early, *parts[1:], near_chips[0], *far_chips)
    parts[1:], near_chips[0], far_chips = rest[:3], rest[3], rest[4:]

    part_out = lax.ppermute(parts[3], "shard", [(0, 3), (3, 0)])
    near_blocks = [(chip, 0) for chip in near_chips + [swap(near_chips[0], "expert", 6)]]
    far_blocks = [(chip, first) for first in (0, rows) for chip in far_chips]
    (late,) = run(far_blocks, slice(0, 1), [])
    (middle,) = run(near_blocks, slice(0, 1), [])
    part_out, late, middle = stage(part_out, late, middle)
    parts[3] = jnp.where(inner, part_in, part_out)
    weights.append(parts)
    others.append([swap(part, "expert", 1) for part in parts])

    sums = {}
    far = run(far_blocks, slice(1, 2), [(late, 0), (late, tile_rows)], "labelled")
    far_x, far_y = swap(far[0], "expert", 2), swap(far[1], "expert", 4)
    close = run(near_blocks + own_blocks, slice(1, 2), [(middle, 0), (after(early, far[2]), 0)], "ordered")
    far_x, far_y, *close = stage(far_x, far_y, *close)
    close_x, close_y = swap(close[0], "expert", 2), swap(close[1], "expert", 4)
    for pair, left, right, a_x, b_y in (
        ((3, 2), far[2], far[3], far_x, far_y), ((1, 0), close[2], close[3], close_x, close_y)
    ):
        a_y = swap(add(left[1], a_x[1]), "expert", 4)
        b_x = swap(add(right[1], b_y[1]), "expert", 2)
        left = left[0].astype(f32) + a_x[0].astype(f32) + a_y.astype(f32)
        right = right[0].astype(f32) + b_y[0].astype(f32) + b_x.astype(f32)
        for i, k in enumerate(pair):
            sums[k] = jnp.concatenate([left[i], right[i]], axis=1)
    sent = [swap(sums[k].astype(bf16), "shard", k) for k in range(1, shards)]
    total = hidden.astype(f32) + sums[0]
    for part in sent:
        total = total + part.astype(f32)
    return rms_scale(total, final_gain).astype(bf16)


def choose_slots(routes, replica_pick, placement, experts):
    labels = jnp.arange(experts, dtype=jnp.int32)
    holder_mask = (placement[None, :] == labels[:, None]).astype(jnp.int32)
    before = jnp.cumsum(holder_mask, axis=1) - holder_mask
    copies = jnp.sum(holder_mask, axis=1)
    places = jnp.arange(placement.shape[0], dtype=jnp.int32)
    route_hits = (routes[..., None] == labels).astype(jnp.int32)
    held_count = jnp.sum(route_hits * copies, axis=-1)
    wanted = replica_pick % held_count
    chosen = jnp.zeros(routes.shape, jnp.int32)
    for replica in range(most_copies):
        column = jnp.sum(
            holder_mask * (before == replica).astype(jnp.int32) * places[None, :], axis=1
        )
        candidate = jnp.sum(route_hits * column, axis=-1)
        chosen = jnp.where(wanted == replica, candidate, chosen)
    return chosen


def padded_experts(inbound, gate_up, down_proj):
    sources, slot_count, slot_depth, model_width = inbound.shape
    per_source = slot_count * slot_depth
    upper_bound = max(1, 1024 // per_source)
    power_two = 1 << upper_bound.bit_length() - 1
    group_size = math.gcd(sources, power_two)
    stacked = inbound.reshape(
        sources // group_size, group_size, slot_count, slot_depth, model_width
    )
    hidden_units = down_proj.shape[1]

    def apply_block(block_part):
        both_parts = jnp.einsum(
            "bjmd,jdf->bjmf", block_part, gate_up, preferred_element_type=jnp.float32
        )
        activated = (
            jax.nn.silu(both_parts[..., :hidden_units]) * both_parts[..., hidden_units:]
        ).astype(jnp.bfloat16)
        return jnp.einsum(
            "bjmf,jfd->bjmd", activated, down_proj, preferred_element_type=jnp.float32
        ).astype(jnp.bfloat16)

    return lax.map(apply_block, stacked).reshape(inbound.shape)


def body(
    head_outputs,
    residual,
    output_weight,
    router,
    norm_gain,
    placed_gate_up,
    placed_down,
    routes,
    replica_pick,
    placement,
    final_gain,
):
    row_count, model_width = residual.shape
    route_count = routes.shape[1]
    experts = router.shape[1]
    place_count = placement.shape[0]
    groups = lax.axis_size("expert")
    slot_count = place_count // groups
    capacity = CAP
    projected = jnp.dot(
        head_outputs,
        lax.all_gather(output_weight, "shard", axis=0, tiled=True),
        preferred_element_type=jnp.float32,
    )
    hidden = (residual.astype(jnp.float32) + projected).astype(jnp.bfloat16)
    hidden_wide = hidden.astype(jnp.float32)
    normed = rms_scale(hidden_wide, norm_gain).astype(jnp.bfloat16)
    logits = jnp.dot(normed, router, preferred_element_type=jnp.float32)
    labels = jnp.arange(experts, dtype=jnp.int32)
    selector = (routes[..., None] == labels).astype(jnp.float32)
    chosen_logits = jnp.sum(selector * logits[:, None, :], axis=-1)
    raised = jnp.exp(chosen_logits)
    route_weight = raised / jnp.sum(raised, axis=-1, keepdims=True)
    slot_ids = choose_slots(routes, replica_pick, placement, experts).reshape(-1)
    slot_hits = (slot_ids[:, None] == jnp.arange(place_count, dtype=jnp.int32)).astype(jnp.int32)
    slot_rank = jnp.sum((jnp.cumsum(slot_hits, axis=0) - slot_hits) * slot_hits, axis=1)
    copies_out = jnp.repeat(normed, route_count, axis=0)
    gate_up, down_proj = (
        lax.all_gather(placed_gate_up, "shard", axis=1, tiled=True),
        lax.all_gather(placed_down, "shard", axis=1, tiled=True),
    )
    buffer_index = slot_ids * capacity + slot_rank
    outbound = (
        jnp.zeros((place_count * capacity, model_width), jnp.bfloat16)
        .at[buffer_index]
        .set(copies_out)
    )
    inbound = lax.all_to_all(
        outbound.reshape(groups, slot_count * capacity, model_width),
        "expert",
        split_axis=0,
        concat_axis=0,
        tiled=True,
    )
    inbound = inbound.reshape(groups, slot_count, capacity, model_width)
    answers = padded_experts(inbound, gate_up, down_proj)
    returned = lax.all_to_all(
        answers.reshape(groups, slot_count * capacity, model_width),
        "expert",
        split_axis=0,
        concat_axis=0,
        tiled=True,
    )
    returned = returned.reshape(place_count * capacity, model_width)
    gathered = returned[buffer_index].reshape(row_count, route_count, model_width)
    mixture = jnp.sum(route_weight[..., None] * gathered.astype(jnp.float32), axis=1)
    return rms_scale(hidden_wide + mixture, final_gain).astype(jnp.bfloat16)


def solution(mesh):
    by_quarters = mesh.shape["expert"] == 8 and mesh.shape["shard"] == 4
    return jax.shard_map(
        quarter_body if by_quarters else body,
        mesh=mesh,
        in_specs=(
            P(("expert", "shard"), None),
            P(("expert", "shard"), None),
            P("shard", None),
            P(),
            P(),
            P("expert", "shard", None),
            P("expert", "shard", None),
            P(("expert", "shard"), None),
            P(("expert", "shard"), None),
            P(),
            P(),
        ),
        out_specs=P(("expert", "shard"), None),
        check_vma=False,
    )
```

```python
import functools
import math

import jax
import jax.numpy as jnp
from jax import lax
from jax.experimental import pallas as pl
from jax.experimental.pallas import tpu as pltpu
from jax.sharding import PartitionSpec as P

CAP = 48


eps_norm = 1e-06
most_copies = 3


def rms_scale(values, scale_gain):
    mean_square = jnp.mean(values * values, axis=-1, keepdims=True)
    return values * lax.rsqrt(mean_square + eps_norm) * scale_gain


bf16 = jnp.bfloat16
f32 = jnp.float32
vmem_limit = 62 * 1024 * 1024
tile_rows = 512
chunks = ((0, 3), (3, 5))
any_space = pl.BlockSpec(memory_space=pl.ANY)
in_vmem = pl.BlockSpec(memory_space=pltpu.VMEM)
in_smem = pl.BlockSpec(memory_space=pltpu.SMEM)


def swap(value, axis, bits):
    size = lax.axis_size(axis)
    return lax.ppermute(value, axis, [(i, i ^ bits) for i in range(size)])


def hit_table(routes, picks, column, row, places):
    lanes = row.shape[1]
    same = column == row
    q = lax.broadcasted_iota(jnp.int32, same.shape, 0)
    p = lax.broadcasted_iota(jnp.int32, same.shape, 1) % places
    copies = jnp.sum(jnp.where(same & (q < places), 1.0, 0.0), axis=0, keepdims=True)
    rank = jnp.sum(jnp.where(same & (q < p), 1.0, 0.0), axis=0, keepdims=True)
    routes = jnp.transpose(routes.astype(f32))
    rests = [jnp.transpose(lax.rem(picks, jnp.full_like(picks, count)).astype(f32)) for count in range(2, most_copies + 1)]
    hits = jnp.zeros((routes.shape[0], lanes), f32)
    for k in range(routes.shape[1]):
        wanted = jnp.zeros(hits.shape, f32)
        for count, rest in enumerate(rests, 2):
            wanted = jnp.where(copies == count, rest[:, k:k + 1], wanted)
        hits = jnp.where((routes[:, k:k + 1] == row) & (wanted == rank), 1.0, hits)
    return hits


def quarters_kernel(weights_ref, send_ref):
    shards, _, columns = send_ref.shape
    units = columns // 2
    for q in range(shards):
        for part in range(2):
            at = (part * shards + q) * units
            send_ref[q, :, part * units:(part + 1) * units] = weights_ref[0, :, at:at + units]


def quarters(weights, first, slots, shards):
    _, depth, columns = weights.shape
    part = columns // shards
    return pl.pallas_call(
        quarters_kernel,
        out_shape=jax.ShapeDtypeStruct((shards, depth, part * slots), bf16),
        grid=(slots,),
        in_specs=[pl.BlockSpec((1, depth, columns), lambda i: (first + i, 0, 0))],
        out_specs=pl.BlockSpec((shards, depth, part), lambda i: (0, 0, i)),
        compiler_params=pltpu.CompilerParams(vmem_limit_bytes=vmem_limit),
        cost_estimate=pl.CostEstimate(flops=0, bytes_accessed=4 * depth * columns * slots, transcendentals=0),
        name="quarters",
    )(weights)


class Loads:
    def __init__(self, sems):
        self.sems = sems
        self.used = 0
        self.waiting = {}

    def start(self, name, source, target):
        copy = pltpu.make_async_copy(source, target, self.sems.at[self.used])
        copy.start()
        self.used += 1
        self.waiting.setdefault(name, []).append(copy)

    def wait(self, name):
        for copy in self.waiting.pop(name, []):
            copy.wait()


def project_kernel(
    where_ref, heads_hbm, residual_hbm, gain_hbm, router_hbm, routes_hbm, picks_hbm, experts_hbm, *refs
):
    pieces = refs[:-11]
    rows_ref, hidden_ref, weight, heads_ref, residual_ref, gain_ref, router_ref = refs[-11:-4]
    routes_ref, picks_ref, experts_ref, sems = refs[-4:]
    e = where_ref[0]
    s = where_ref[1]
    chips = len(pieces) // 2
    shards, piece, _ = pieces[0].shape
    depth = weight.shape[0] // shards
    loads = Loads(sems)
    for source, target in (
        (routes_hbm, routes_ref), (picks_hbm, picks_ref), (experts_hbm, experts_ref), (router_hbm, router_ref),
    ):
        loads.start("routing", source, target)
    for core in range(2):
        for chip in range(chips):
            for k in range(shards):
                start = pl.multiple_of((s ^ k) * depth + (e ^ (2 * chip + core)) * piece, piece)
                loads.start("weight", pieces[core * chips + chip].at[k], weight.at[pl.ds(start, piece), :])
    for source, target in ((heads_hbm, heads_ref), (residual_hbm, residual_ref), (gain_hbm, gain_ref)):
        loads.start("weight", source, target)
    loads.wait("routing")
    places = experts_ref.shape[1]
    row = experts_ref[...].astype(f32)
    row = jnp.concatenate([row, row], axis=1)
    column = jnp.transpose(jnp.broadcast_to(row, (row.shape[1], row.shape[1])))
    hits = hit_table(routes_ref[...], picks_ref[...], column, row, places)
    count = router_ref.shape[0]
    label = lax.broadcasted_iota(jnp.int32, (row.shape[1], count), 1).astype(f32)
    chosen = jnp.where(column[:, :count] == label, 1.0, 0.0).astype(bf16)
    router = jnp.dot(chosen, router_ref[...], preferred_element_type=f32).astype(bf16)
    loads.wait("weight")
    projected = jnp.dot(heads_ref[...], weight[...], preferred_element_type=f32)
    hidden = (residual_ref[...].astype(f32) + projected).astype(bf16)
    hidden_ref[...] = hidden
    normed = rms_scale(hidden.astype(f32), gain_ref[...]).astype(bf16)
    width = normed.shape[1]
    rows_ref[:, :width] = normed
    logits = lax.dot_general(normed, router, (((1,), (1,)), ((), ())), preferred_element_type=f32)
    raised = jnp.where(hits > 0, jnp.exp(logits), 0.0)
    total = jnp.sum(raised, axis=-1, keepdims=True) * 0.5
    share = raised / total
    high = share.astype(bf16)
    low = (share - high.astype(f32)).astype(bf16)
    lane = lax.broadcasted_iota(jnp.int32, share.shape, 1)
    rows_ref[:, width:] = jnp.where(lane < places, high.astype(f32), low.astype(f32)).astype(bf16)


def project(where, heads, residual, gain, router, routes, picks, placement, pieces):
    rows, width = residual.shape
    pairs = 2 * placement.shape[0]
    places = placement.shape[0]
    operands = (
        heads, residual, gain.reshape(1, -1), router.T, routes.T, picks.T, placement.reshape(1, -1), *pieces,
    )
    count = len(operands) + len(pieces) * (pieces[0].shape[0] - 1)
    return pl.pallas_call(
        project_kernel,
        out_shape=(
            jax.ShapeDtypeStruct((rows, width + pairs), bf16),
            jax.ShapeDtypeStruct((rows, width), bf16),
        ),
        in_specs=[in_smem] + [any_space] * len(operands),
        out_specs=(in_vmem, in_vmem),
        scratch_shapes=[
            pltpu.VMEM((width, width), bf16),
            pltpu.VMEM((rows, width), bf16),
            pltpu.VMEM((rows, width), bf16),
            pltpu.VMEM((1, width), f32),
            pltpu.VMEM(router.shape[::-1], bf16),
            pltpu.VMEM(routes.shape[::-1], jnp.int32),
            pltpu.VMEM(picks.shape[::-1], jnp.int32),
            pltpu.VMEM((1, places), jnp.int32),
            pltpu.SemaphoreType.DMA((count,)),
        ],
        compiler_params=pltpu.CompilerParams(vmem_limit_bytes=vmem_limit),
        cost_estimate=pl.CostEstimate(
            flops=2 * rows * width * width, bytes_accessed=3 * width * width, transcendentals=rows * pairs
        ),
        name="project",
    )(where, *operands)


def activate(both, shares, first, slots):
    units = shares.shape[1]
    pairs = shares.shape[1]
    place = lax.broadcasted_iota(jnp.int32, (pairs, slots * units), 0) % (pairs // 2)
    lane = lax.broadcasted_iota(jnp.int32, (pairs, slots * units), 1) // units
    spread = jnp.where(place == lane + first, 1.0, 0.0).astype(bf16)
    factor = jnp.dot(shares, spread, preferred_element_type=f32)
    parts = []
    for slot in range(slots):
        gate = both[:, 2 * slot * units:(2 * slot + 1) * units]
        up = both[:, (2 * slot + 1) * units:(2 * slot + 2) * units]
        act = gate / (1.0 + jnp.exp(-gate)) * up
        parts.append((act * factor[:, slot * units:(slot + 1) * units]).astype(bf16))
    return parts


def slots_kernel(slot_sets, group_slots, block_rows, source_counts, sum_rows, cut, where_ref, *refs):
    refs = list(refs)

    def take(count):
        taken, refs[:] = refs[:count], refs[count:]
        return taken

    block_count, has_sums = len(block_rows), bool(sum_rows)
    blocks = take(block_count)
    sources = [take(count) for count in source_counts]
    downs = take(2)
    earlier = take(len(sum_rows))
    outs = take(4 if cut else 1)
    sets = len(slot_sets)
    weights = take(sets)
    x, total, act, down, weight_sems, x_sems, sum_sems, out_sems = refs
    tiles, tile_rows, _ = x.shape
    width = weights[0].shape[0]
    units = x.shape[2] - width

    def load_weights(i):
        if len(sources[i]) == 1:
            blocks = [sources[i][0].at[q] for q in range(sources[i][0].shape[0])]
        else:
            blocks = sources[i]
        for k, block in enumerate(blocks):
            depth = block.shape[0]
            last = min(k, 3)
            q = k if len(sources[i]) == 1 else where_ref[1] ^ last
            target = weights[i].at[pl.ds(pl.multiple_of(q * depth, depth), depth), :]
            copy = pltpu.make_async_copy(block, target, weight_sems.at[i])
            if len(sources[i]) == 1 or k < 3:
                copy.start()
            else:
                pl.when(where_ref[2] == (1 if k == 3 else 0))(copy.start)

    def load_tile(tile):
        rows = tiles * tile_rows // block_count
        for i, (block, first) in enumerate(zip(blocks, block_rows)):
            if i * rows // tile_rows == tile:
                target = x.at[tile, pl.ds(i * rows % tile_rows, rows), :]
                pltpu.make_async_copy(block.at[pl.ds(first, rows), :], target, x_sems.at[tile]).start()

    load_weights(0)
    for tile in range(tiles):
        load_tile(tile)
    for i in range(1, sets):
        load_weights(i)
    at = 0
    for flip, first, count in slot_sets:
        source, target = downs[flip].at[pl.ds(first * units, count * units), :], down.at[pl.ds(at, count * units), :]
        pltpu.make_async_copy(source, target, weight_sems.at[sets]).start()
        at += count * units
    for tile in range(tiles):
        if has_sums:
            source = earlier[tile].at[pl.ds(sum_rows[tile], tile_rows), :]
            pltpu.make_async_copy(source, total.at[tile], sum_sems.at[tile]).start()

    at = 0
    for i, (flip, first, count) in enumerate(slot_sets):
        pltpu.make_async_copy(weights[i], weights[i], weight_sems.at[i]).wait()
        place = (where_ref[0] ^ flip) * group_slots + first

        @pl.loop(0, tiles)
        def _(tile, i=i, at=at, count=count, place=place):
            if i == 0:
                pltpu.make_async_copy(x.at[tile], x.at[tile], x_sems.at[tile]).wait()
            both = jnp.dot(x[tile, :, :width], weights[i][...], preferred_element_type=f32)
            parts = activate(both, x[tile, :, width:], place, count)
            act[tile, :, at:at + count * units] = jnp.concatenate(parts, axis=1)

        at += count * units
    pltpu.make_async_copy(down, down, weight_sems.at[sets]).wait()

    @pl.loop(0, tiles)
    def _(tile):
        added = jnp.dot(act[tile], down[...], preferred_element_type=f32)
        if has_sums:
            pltpu.make_async_copy(total.at[tile], total.at[tile], sum_sems.at[tile]).wait()
            added = added + total[tile].astype(f32)
        total[tile] = added.astype(bf16)
        if not cut:
            target = outs[0].at[pl.ds(tile * tile_rows, tile_rows), :]
            pltpu.make_async_copy(total.at[tile], target, out_sems.at[tile]).start()

    if cut:
        rows, half = tiles * tile_rows // block_count, width // 2
        parts = block_count // 4
        copies = []
        for part in range(parts):
            place = part if cut == "ordered" else part ^ (1 - where_ref[2])
            for out, chips, column in zip(outs, ((1, 3), (2, 3), (0, 2), (0, 1)), (0, half, 0, half)):
                for i, chip in enumerate(chips):
                    tile, at = divmod((4 * part + chip) * rows, tile_rows)
                    source = total.at[tile, pl.ds(at, rows), pl.ds(column, half)]
                    target = out.at[i, place]
                    copies.append(pltpu.make_async_copy(source, target, out_sems.at[len(copies)]))
        for copy in copies:
            copy.start()
        for copy in copies:
            copy.wait()
    else:
        @pl.loop(0, tiles)
        def _(tile):
            target = outs[0].at[pl.ds(tile * tile_rows, tile_rows), :]
            pltpu.make_async_copy(total.at[tile], target, out_sems.at[tile]).wait()


def slots_block(where, tokens, blocks, sources, slot_sets, downs, earlier, group_slots, cut=None):
    block_rows = tuple(first for _, first in blocks)
    sum_rows = tuple(first for _, first in earlier)
    blocks, earlier = [block for block, _ in blocks], [total for total, _ in earlier]
    rows, wide = len(blocks) * tokens, blocks[0].shape[1]
    width = downs[0].shape[1]
    wides = [source[0].shape[-1] for source in sources]
    columns = sum(wides)
    source_counts = tuple(len(source) for source in sources)
    sources = [block for source in sources for block in source]
    tiles = rows // tile_rows
    if cut:
        out_shape = [jax.ShapeDtypeStruct((2, len(blocks) // 4, tokens, width // 2), bf16)] * 4
    else:
        out_shape = [jax.ShapeDtypeStruct((rows, width), bf16)]
    return pl.pallas_call(
        functools.partial(slots_kernel, slot_sets, group_slots, block_rows, source_counts, sum_rows, cut),
        out_shape=out_shape,
        in_specs=[in_smem] + [any_space] * (len(blocks) + len(sources) + 2 + len(earlier)),
        out_specs=[any_space] * len(out_shape),
        scratch_shapes=[pltpu.VMEM((width, columns), bf16) for columns in wides]
        + [
            pltpu.VMEM((tiles, tile_rows, wide), bf16),
            pltpu.VMEM((tiles, tile_rows, width), bf16),
            pltpu.VMEM((tiles, tile_rows, columns // 2), bf16),
            pltpu.VMEM((columns // 2, width), bf16),
            pltpu.SemaphoreType.DMA((len(wides) + 1,)),
            pltpu.SemaphoreType.DMA((tiles,)),
            pltpu.SemaphoreType.DMA((tiles,)),
            pltpu.SemaphoreType.DMA((max(tiles, 2 * len(blocks)),)),
        ],
        compiler_params=pltpu.CompilerParams(vmem_limit_bytes=vmem_limit),
        cost_estimate=pl.CostEstimate(
            flops=3 * rows * columns * width,
            bytes_accessed=2 * rows * (wide + 2 * width) + 3 * columns * width,
            transcendentals=rows * columns // 2,
        ),
        name="slots_block",
    )(where, *blocks, *sources, *downs, *earlier)


def after(value, *events):
    return lax.optimization_barrier((value, *events))[0]


def chip_gather(block):
    return [block] + [swap(block, "expert", bits) for bits in (2, 4, 6)]


def core_gather(chips):
    return chips + [swap(chip, "expert", 1) for chip in chips]


def stage(*values):
    return lax.optimization_barrier(values)


def add(left, right):
    return (left.astype(f32) + right.astype(f32)).astype(bf16)


def quarter_body(
    head_outputs,
    residual,
    output_weight,
    router,
    norm_gain,
    placed_gate_up,
    placed_down,
    routes,
    replica_pick,
    placement,
    final_gain,
):
    rows, width = residual.shape
    slots, depth, columns = placed_gate_up.shape
    devices, shards = lax.axis_size("expert"), lax.axis_size("shard")
    e, s = lax.axis_index("expert"), lax.axis_index("shard")
    inner = (s == 1) | (s == 2)
    where = jnp.stack([e, s, inner]).astype(jnp.int32)
    hidden_units = columns // 2
    units = hidden_units // shards

    piece = output_weight.shape[0] // devices
    own = lax.dynamic_slice_in_dim(output_weight, e * piece, piece, 0)
    over_z = jnp.stack([own] + [swap(own, "shard", k) for k in range(1, shards)])

    sends = [quarters(placed_gate_up, *chunks[0], shards)]

    def exchange(send):
        return lax.all_to_all(send, "shard", split_axis=0, concat_axis=0, tiled=True)

    over_z, send = stage(over_z, sends[0])
    weights = [exchange(send)]
    down = placed_down.reshape(slots * units, width)
    pieces = chip_gather(over_z)
    sends.append(quarters(after(placed_gate_up, pieces[1]), *chunks[1], shards))
    *pieces, other_down, sends[1] = stage(*pieces, swap(after(down, over_z), "expert", 1), sends[1])
    pieces = core_gather(pieces)
    downs = [down, other_down]
    block, hidden = project(where, head_outputs, residual, norm_gain, router, routes, replica_pick, placement, pieces)

    cross = [(1, 2), (2, 1)]
    outward = [(1, 0), (2, 3)]

    own_chips = chip_gather(block)
    near = swap(block, "shard", 1)
    first_in = lax.ppermute(block, "shard", cross)
    second_in = lax.ppermute(near, "shard", cross)
    parts = [lax.dynamic_index_in_dim(sends[1], s ^ k, 0, keepdims=False) for k in range(shards)]
    near, first_in, second_in, *rest = stage(near, first_in, second_in, *parts, *own_chips)
    parts, own_chips = rest[:4], rest[4:]

    near_chips = [near, swap(near, "expert", 2), swap(near, "expert", 4)]
    first_out = lax.ppermute(first_in, "shard", outward)
    second_out = lax.ppermute(second_in, "shard", outward)
    part_in = lax.ppermute(parts[3], "shard", cross)
    first_out, second_out, weights[0], part_in, *rest = stage(
        first_out, second_out, weights[0], part_in, *parts, *near_chips
    )
    parts, near_chips = list(rest[:4]), list(rest[4:])

    parts[1] = swap(parts[1], "shard", 1)
    parts[2] = swap(parts[2], "shard", 2)
    far = jnp.concatenate([jnp.where(inner, first_in, first_out), jnp.where(inner, second_in, second_out)])
    far_chips = chip_gather(far)

    weights = [[weights[0]]]
    others = [[swap(weights[0][0], "expert", 1)]]
    def run(blocks, which, earlier, cut=None):
        sources, sets = [], []
        for chunk in range(len(chunks))[which]:
            sources += [weights[chunk], others[chunk]]
            sets += [(0, *chunks[chunk]), (1, *chunks[chunk])]
        return slots_block(where, rows, blocks, sources, tuple(sets), downs, earlier, slots, cut)

    own_blocks = [(chip, 0) for chip in own_chips]
    (early,) = run(own_blocks, slice(0, 1), [])
    early, *rest = stage(early, *parts[1:], near_chips[0], *far_chips)
    parts[1:], near_chips[0], far_chips = rest[:3], rest[3], rest[4:]

    part_out = lax.ppermute(parts[3], "shard", [(0, 3), (3, 0)])
    near_blocks = [(chip, 0) for chip in near_chips + [swap(near_chips[0], "expert", 6)]]
    far_blocks = [(chip, first) for first in (0, rows) for chip in far_chips]
    (late,) = run(far_blocks, slice(0, 1), [])
    (middle,) = run(near_blocks, slice(0, 1), [])
    part_out, late, middle = stage(part_out, late, middle)
    parts[3:] = [part_in, part_out]
    weights.append(parts)
    others.append([swap(part, "expert", 1) for part in parts])

    sums = {}
    far = run(far_blocks, slice(1, 2), [(late, 0), (late, tile_rows)], "labelled")
    far_x, far_y = swap(far[0], "expert", 2), swap(far[1], "expert", 4)
    close = run(near_blocks + own_blocks, slice(1, 2), [(middle, 0), (after(early, far[2]), 0)], "ordered")
    far_x, far_y, *close = stage(far_x, far_y, *close)
    close_x, close_y = swap(close[0], "expert", 2), swap(close[1], "expert", 4)
    for pair, left, right, a_x, b_y in (
        ((3, 2), far[2], far[3], far_x, far_y), ((1, 0), close[2], close[3], close_x, close_y)
    ):
        a_y = swap(add(left[1], a_x[1]), "expert", 4)
        b_x = swap(add(right[1], b_y[1]), "expert", 2)
        left = left[0].astype(f32) + a_x[0].astype(f32) + a_y.astype(f32)
        right = right[0].astype(f32) + b_y[0].astype(f32) + b_x.astype(f32)
        for i, k in enumerate(pair):
            sums[k] = jnp.concatenate([left[i], right[i]], axis=1)
    sent = [swap(sums[k].astype(bf16), "shard", k) for k in range(1, shards)]
    total = hidden.astype(f32) + sums[0]
    for part in sent:
        total = total + part.astype(f32)
    return rms_scale(total, final_gain).astype(bf16)


def choose_slots(routes, replica_pick, placement, experts):
    labels = jnp.arange(experts, dtype=jnp.int32)
    holder_mask = (placement[None, :] == labels[:, None]).astype(jnp.int32)
    before = jnp.cumsum(holder_mask, axis=1) - holder_mask
    copies = jnp.sum(holder_mask, axis=1)
    places = jnp.arange(placement.shape[0], dtype=jnp.int32)
    route_hits = (routes[..., None] == labels).astype(jnp.int32)
    held_count = jnp.sum(route_hits * copies, axis=-1)
    wanted = replica_pick % held_count
    chosen = jnp.zeros(routes.shape, jnp.int32)
    for replica in range(most_copies):
        column = jnp.sum(
            holder_mask * (before == replica).astype(jnp.int32) * places[None, :], axis=1
        )
        candidate = jnp.sum(route_hits * column, axis=-1)
        chosen = jnp.where(wanted == replica, candidate, chosen)
    return chosen


def padded_experts(inbound, gate_up, down_proj):
    sources, slot_count, slot_depth, model_width = inbound.shape
    per_source = slot_count * slot_depth
    upper_bound = max(1, 1024 // per_source)
    power_two = 1 << upper_bound.bit_length() - 1
    group_size = math.gcd(sources, power_two)
    stacked = inbound.reshape(
        sources // group_size, group_size, slot_count, slot_depth, model_width
    )
    hidden_units = down_proj.shape[1]

    def apply_block(block_part):
        both_parts = jnp.einsum(
            "bjmd,jdf->bjmf", block_part, gate_up, preferred_element_type=jnp.float32
        )
        activated = (
            jax.nn.silu(both_parts[..., :hidden_units]) * both_parts[..., hidden_units:]
        ).astype(jnp.bfloat16)
        return jnp.einsum(
            "bjmf,jfd->bjmd", activated, down_proj, preferred_element_type=jnp.float32
        ).astype(jnp.bfloat16)

    return lax.map(apply_block, stacked).reshape(inbound.shape)


def body(
    head_outputs,
    residual,
    output_weight,
    router,
    norm_gain,
    placed_gate_up,
    placed_down,
    routes,
    replica_pick,
    placement,
    final_gain,
):
    row_count, model_width = residual.shape
    route_count = routes.shape[1]
    experts = router.shape[1]
    place_count = placement.shape[0]
    groups = lax.axis_size("expert")
    slot_count = place_count // groups
    capacity = CAP
    projected = jnp.dot(
        head_outputs,
        lax.all_gather(output_weight, "shard", axis=0, tiled=True),
        preferred_element_type=jnp.float32,
    )
    hidden = (residual.astype(jnp.float32) + projected).astype(jnp.bfloat16)
    hidden_wide = hidden.astype(jnp.float32)
    normed = rms_scale(hidden_wide, norm_gain).astype(jnp.bfloat16)
    logits = jnp.dot(normed, router, preferred_element_type=jnp.float32)
    labels = jnp.arange(experts, dtype=jnp.int32)
    selector = (routes[..., None] == labels).astype(jnp.float32)
    chosen_logits = jnp.sum(selector * logits[:, None, :], axis=-1)
    raised = jnp.exp(chosen_logits)
    route_weight = raised / jnp.sum(raised, axis=-1, keepdims=True)
    slot_ids = choose_slots(routes, replica_pick, placement, experts).reshape(-1)
    slot_hits = (slot_ids[:, None] == jnp.arange(place_count, dtype=jnp.int32)).astype(jnp.int32)
    slot_rank = jnp.sum((jnp.cumsum(slot_hits, axis=0) - slot_hits) * slot_hits, axis=1)
    copies_out = jnp.repeat(normed, route_count, axis=0)
    gate_up, down_proj = (
        lax.all_gather(placed_gate_up, "shard", axis=1, tiled=True),
        lax.all_gather(placed_down, "shard", axis=1, tiled=True),
    )
    buffer_index = slot_ids * capacity + slot_rank
    outbound = (
        jnp.zeros((place_count * capacity, model_width), jnp.bfloat16)
        .at[buffer_index]
        .set(copies_out)
    )
    inbound = lax.all_to_all(
        outbound.reshape(groups, slot_count * capacity, model_width),
        "expert",
        split_axis=0,
        concat_axis=0,
        tiled=True,
    )
    inbound = inbound.reshape(groups, slot_count, capacity, model_width)
    answers = padded_experts(inbound, gate_up, down_proj)
    returned = lax.all_to_all(
        answers.reshape(groups, slot_count * capacity, model_width),
        "expert",
        split_axis=0,
        concat_axis=0,
        tiled=True,
    )
    returned = returned.reshape(place_count * capacity, model_width)
    gathered = returned[buffer_index].reshape(row_count, route_count, model_width)
    mixture = jnp.sum(route_weight[..., None] * gathered.astype(jnp.float32), axis=1)
    return rms_scale(hidden_wide + mixture, final_gain).astype(jnp.bfloat16)


def solution(mesh):
    by_quarters = mesh.shape["expert"] == 8 and mesh.shape["shard"] == 4
    return jax.shard_map(
        quarter_body if by_quarters else body,
        mesh=mesh,
        in_specs=(
            P(("expert", "shard"), None),
            P(("expert", "shard"), None),
            P("shard", None),
            P(),
            P(),
            P("expert", "shard", None),
            P("expert", "shard", None),
            P(("expert", "shard"), None),
            P(("expert", "shard"), None),
            P(),
            P(),
        ),
        out_specs=P(("expert", "shard"), None),
        check_vma=False,
    )
```

```python
import functools
import math

import jax
import jax.numpy as jnp
from jax import lax
from jax.experimental import pallas as pl
from jax.experimental.pallas import tpu as pltpu
from jax.sharding import PartitionSpec as P

CAP = 48


eps_norm = 1e-06
most_copies = 3


def rms_scale(values, scale_gain):
    mean_square = jnp.mean(values * values, axis=-1, keepdims=True)
    return values * lax.rsqrt(mean_square + eps_norm) * scale_gain


bf16 = jnp.bfloat16
f32 = jnp.float32
vmem_limit = 62 * 1024 * 1024
tile_rows = 512
chunks = ((0, 3), (3, 5))
any_space = pl.BlockSpec(memory_space=pl.ANY)
in_vmem = pl.BlockSpec(memory_space=pltpu.VMEM)
in_smem = pl.BlockSpec(memory_space=pltpu.SMEM)


def swap(value, axis, bits):
    size = lax.axis_size(axis)
    return lax.ppermute(value, axis, [(i, i ^ bits) for i in range(size)])


def hit_table(routes, picks, column, row, places):
    lanes = row.shape[1]
    same = column == row
    q = lax.broadcasted_iota(jnp.int32, same.shape, 0)
    p = lax.broadcasted_iota(jnp.int32, same.shape, 1) % places
    copies = jnp.sum(jnp.where(same & (q < places), 1.0, 0.0), axis=0, keepdims=True)
    rank = jnp.sum(jnp.where(same & (q < p), 1.0, 0.0), axis=0, keepdims=True)
    routes = jnp.transpose(routes.astype(f32))
    rests = [jnp.transpose(lax.rem(picks, jnp.full_like(picks, count)).astype(f32)) for count in range(2, most_copies + 1)]
    hits = jnp.zeros((routes.shape[0], lanes), f32)
    for k in range(routes.shape[1]):
        wanted = jnp.zeros(hits.shape, f32)
        for count, rest in enumerate(rests, 2):
            wanted = jnp.where(copies == count, rest[:, k:k + 1], wanted)
        hits = jnp.where((routes[:, k:k + 1] == row) & (wanted == rank), 1.0, hits)
    return hits


def quarters_kernel(weights_ref, send_ref):
    shards, _, columns = send_ref.shape
    units = columns // 2
    for q in range(shards):
        for part in range(2):
            at = (part * shards + q) * units
            send_ref[q, :, part * units:(part + 1) * units] = weights_ref[0, :, at:at + units]


def quarters(weights, first, slots, shards):
    _, depth, columns = weights.shape
    part = columns // shards
    return pl.pallas_call(
        quarters_kernel,
        out_shape=jax.ShapeDtypeStruct((shards, depth, part * slots), bf16),
        grid=(slots,),
        in_specs=[pl.BlockSpec((1, depth, columns), lambda i: (first + i, 0, 0))],
        out_specs=pl.BlockSpec((shards, depth, part), lambda i: (0, 0, i)),
        compiler_params=pltpu.CompilerParams(vmem_limit_bytes=vmem_limit),
        cost_estimate=pl.CostEstimate(flops=0, bytes_accessed=4 * depth * columns * slots, transcendentals=0),
        name="quarters",
    )(weights)


class Loads:
    def __init__(self, sems):
        self.sems = sems
        self.used = 0
        self.waiting = {}

    def start(self, name, source, target):
        copy = pltpu.make_async_copy(source, target, self.sems.at[self.used])
        copy.start()
        self.used += 1
        self.waiting.setdefault(name, []).append(copy)

    def wait(self, name):
        for copy in self.waiting.pop(name, []):
            copy.wait()


def project_kernel(
    where_ref, heads_hbm, residual_hbm, gain_hbm, router_hbm, routes_hbm, picks_hbm, experts_hbm, *refs
):
    pieces = refs[:-11]
    rows_ref, hidden_ref, weight, heads_ref, residual_ref, gain_ref, router_ref = refs[-11:-4]
    routes_ref, picks_ref, experts_ref, sems = refs[-4:]
    e = where_ref[0]
    s = where_ref[1]
    chips = len(pieces) // 2
    shards, piece, _ = pieces[0].shape
    depth = weight.shape[0] // shards
    loads = Loads(sems)
    for source, target in (
        (routes_hbm, routes_ref), (picks_hbm, picks_ref), (experts_hbm, experts_ref), (router_hbm, router_ref),
    ):
        loads.start("routing", source, target)
    for core in range(2):
        for chip in range(chips):
            for k in range(shards):
                start = pl.multiple_of((s ^ k) * depth + (e ^ (2 * chip + core)) * piece, piece)
                loads.start("weight", pieces[core * chips + chip].at[k], weight.at[pl.ds(start, piece), :])
    for source, target in ((heads_hbm, heads_ref), (residual_hbm, residual_ref), (gain_hbm, gain_ref)):
        loads.start("weight", source, target)
    loads.wait("routing")
    places = experts_ref.shape[1]
    row = experts_ref[...].astype(f32)
    row = jnp.concatenate([row, row], axis=1)
    column = jnp.transpose(jnp.broadcast_to(row, (row.shape[1], row.shape[1])))
    hits = hit_table(routes_ref[...], picks_ref[...], column, row, places)
    count = router_ref.shape[0]
    label = lax.broadcasted_iota(jnp.int32, (row.shape[1], count), 1).astype(f32)
    chosen = jnp.where(column[:, :count] == label, 1.0, 0.0).astype(bf16)
    router = jnp.dot(chosen, router_ref[...], preferred_element_type=f32).astype(bf16)
    loads.wait("weight")
    projected = jnp.dot(heads_ref[...], weight[...], preferred_element_type=f32)
    hidden = (residual_ref[...].astype(f32) + projected).astype(bf16)
    hidden_ref[...] = hidden
    normed = rms_scale(hidden.astype(f32), gain_ref[...]).astype(bf16)
    width = normed.shape[1]
    rows_ref[:, :width] = normed
    logits = lax.dot_general(normed, router, (((1,), (1,)), ((), ())), preferred_element_type=f32)
    raised = jnp.where(hits > 0, jnp.exp(logits), 0.0)
    total = jnp.sum(raised, axis=-1, keepdims=True) * 0.5
    share = raised / total
    high = share.astype(bf16)
    low = (share - high.astype(f32)).astype(bf16)
    lane = lax.broadcasted_iota(jnp.int32, share.shape, 1)
    rows_ref[:, width:] = jnp.where(lane < places, high.astype(f32), low.astype(f32)).astype(bf16)


def project(where, heads, residual, gain, router, routes, picks, placement, pieces):
    rows, width = residual.shape
    pairs = 2 * placement.shape[0]
    places = placement.shape[0]
    operands = (
        heads, residual, gain.reshape(1, -1), router.T, routes.T, picks.T, placement.reshape(1, -1), *pieces,
    )
    count = len(operands) + len(pieces) * (pieces[0].shape[0] - 1)
    return pl.pallas_call(
        project_kernel,
        out_shape=(
            jax.ShapeDtypeStruct((rows, width + pairs), bf16),
            jax.ShapeDtypeStruct((rows, width), bf16),
        ),
        in_specs=[in_smem] + [any_space] * len(operands),
        out_specs=(in_vmem, in_vmem),
        scratch_shapes=[
            pltpu.VMEM((width, width), bf16),
            pltpu.VMEM((rows, width), bf16),
            pltpu.VMEM((rows, width), bf16),
            pltpu.VMEM((1, width), f32),
            pltpu.VMEM(router.shape[::-1], bf16),
            pltpu.VMEM(routes.shape[::-1], jnp.int32),
            pltpu.VMEM(picks.shape[::-1], jnp.int32),
            pltpu.VMEM((1, places), jnp.int32),
            pltpu.SemaphoreType.DMA((count,)),
        ],
        compiler_params=pltpu.CompilerParams(vmem_limit_bytes=vmem_limit),
        cost_estimate=pl.CostEstimate(
            flops=2 * rows * width * width, bytes_accessed=3 * width * width, transcendentals=rows * pairs
        ),
        name="project",
    )(where, *operands)


def activate(both, shares, first, slots):
    units = shares.shape[1]
    pairs = shares.shape[1]
    place = lax.broadcasted_iota(jnp.int32, (pairs, slots * units), 0) % (pairs // 2)
    lane = lax.broadcasted_iota(jnp.int32, (pairs, slots * units), 1) // units
    spread = jnp.where(place == lane + first, 1.0, 0.0).astype(bf16)
    factor = jnp.dot(shares, spread, preferred_element_type=f32)
    parts = []
    for slot in range(slots):
        gate = both[:, 2 * slot * units:(2 * slot + 1) * units]
        up = both[:, (2 * slot + 1) * units:(2 * slot + 2) * units]
        act = gate / (1.0 + jnp.exp(-gate)) * up
        parts.append((act * factor[:, slot * units:(slot + 1) * units]).astype(bf16))
    return parts


def slots_kernel(slot_sets, group_slots, block_rows, source_counts, sum_rows, cut, where_ref, *refs):
    refs = list(refs)

    def take(count):
        taken, refs[:] = refs[:count], refs[count:]
        return taken

    block_count, has_sums = len(block_rows), bool(sum_rows)
    blocks = take(block_count)
    sources = [take(count) for count in source_counts]
    downs = take(2)
    earlier = take(len(sum_rows))
    outs = take(4 if cut else 1)
    sets = len(slot_sets)
    weights = take(sets)
    x, total, act, down, weight_sems, x_sems, sum_sems, out_sems = refs
    tiles, tile_rows, _ = x.shape
    width = weights[0].shape[0]
    units = x.shape[2] - width

    def load_weights(i):
        if len(sources[i]) == 1:
            blocks = [sources[i][0].at[q] for q in range(sources[i][0].shape[0])]
        else:
            blocks = sources[i]
        for k, block in enumerate(blocks):
            depth = block.shape[0]
            last = min(k, 3)
            q = k if len(sources[i]) == 1 else where_ref[1] ^ last
            target = weights[i].at[pl.ds(pl.multiple_of(q * depth, depth), depth), :]
            copy = pltpu.make_async_copy(block, target, weight_sems.at[i])
            if len(sources[i]) == 1 or k < 3:
                copy.start()
            else:
                pl.when(where_ref[2] == (1 if k == 3 else 0))(copy.start)

    def load_tile(tile):
        rows = tiles * tile_rows // block_count
        for i, (block, first) in enumerate(zip(blocks, block_rows)):
            if i * rows // tile_rows == tile:
                target = x.at[tile, pl.ds(i * rows % tile_rows, rows), :]
                pltpu.make_async_copy(block.at[pl.ds(first, rows), :], target, x_sems.at[tile]).start()

    load_weights(0)
    for tile in range(tiles):
        load_tile(tile)
    for i in range(1, sets):
        load_weights(i)
    at = 0
    for flip, first, count in slot_sets:
        source, target = downs[flip].at[pl.ds(first * units, count * units), :], down.at[pl.ds(at, count * units), :]
        pltpu.make_async_copy(source, target, weight_sems.at[sets]).start()
        at += count * units
    for tile in range(tiles):
        if has_sums:
            source = earlier[tile].at[pl.ds(sum_rows[tile], tile_rows), :]
            pltpu.make_async_copy(source, total.at[tile], sum_sems.at[tile]).start()

    at = 0
    for i, (flip, first, count) in enumerate(slot_sets):
        pltpu.make_async_copy(weights[i], weights[i], weight_sems.at[i]).wait()
        place = (where_ref[0] ^ flip) * group_slots + first

        @pl.loop(0, tiles)
        def _(tile, i=i, at=at, count=count, place=place):
            if i == 0:
                pltpu.make_async_copy(x.at[tile], x.at[tile], x_sems.at[tile]).wait()
            both = jnp.dot(x[tile, :, :width], weights[i][...], preferred_element_type=f32)
            parts = activate(both, x[tile, :, width:], place, count)
            act[tile, :, at:at + count * units] = jnp.concatenate(parts, axis=1)

        at += count * units
    pltpu.make_async_copy(down, down, weight_sems.at[sets]).wait()

    @pl.loop(0, tiles)
    def _(tile):
        added = jnp.dot(act[tile], down[...], preferred_element_type=f32)
        if has_sums:
            pltpu.make_async_copy(total.at[tile], total.at[tile], sum_sems.at[tile]).wait()
            added = added + total[tile].astype(f32)
        total[tile] = added.astype(bf16)
        if not cut:
            target = outs[0].at[pl.ds(tile * tile_rows, tile_rows), :]
            pltpu.make_async_copy(total.at[tile], target, out_sems.at[tile]).start()

    if cut:
        rows, half = tiles * tile_rows // block_count, width // 2
        parts = block_count // 4
        copies = []
        for part in range(parts):
            place = part if cut == "ordered" else part ^ (1 - where_ref[2])
            for out, chips, column in zip(outs, ((1, 3), (2, 3), (0, 2), (0, 1)), (0, half, 0, half)):
                for i, chip in enumerate(chips):
                    tile, at = divmod((4 * part + chip) * rows, tile_rows)
                    source = total.at[tile, pl.ds(at, rows), pl.ds(column, half)]
                    target = out.at[i, place]
                    copies.append(pltpu.make_async_copy(source, target, out_sems.at[len(copies)]))
        for copy in copies:
            copy.start()
        for copy in copies:
            copy.wait()
    else:
        @pl.loop(0, tiles)
        def _(tile):
            target = outs[0].at[pl.ds(tile * tile_rows, tile_rows), :]
            pltpu.make_async_copy(total.at[tile], target, out_sems.at[tile]).wait()


def slots_block(where, tokens, blocks, sources, slot_sets, downs, earlier, group_slots, cut=None):
    block_rows = tuple(first for _, first in blocks)
    sum_rows = tuple(first for _, first in earlier)
    blocks, earlier = [block for block, _ in blocks], [total for total, _ in earlier]
    rows, wide = len(blocks) * tokens, blocks[0].shape[1]
    width = downs[0].shape[1]
    wides = [source[0].shape[-1] for source in sources]
    columns = sum(wides)
    source_counts = tuple(len(source) for source in sources)
    sources = [block for source in sources for block in source]
    tiles = rows // tile_rows
    if cut:
        out_shape = [jax.ShapeDtypeStruct((2, len(blocks) // 4, tokens, width // 2), bf16)] * 4
    else:
        out_shape = [jax.ShapeDtypeStruct((rows, width), bf16)]
    return pl.pallas_call(
        functools.partial(slots_kernel, slot_sets, group_slots, block_rows, source_counts, sum_rows, cut),
        out_shape=out_shape,
        in_specs=[in_smem] + [any_space] * (len(blocks) + len(sources) + 2 + len(earlier)),
        out_specs=[any_space] * len(out_shape),
        scratch_shapes=[pltpu.VMEM((width, columns), bf16) for columns in wides]
        + [
            pltpu.VMEM((tiles, tile_rows, wide), bf16),
            pltpu.VMEM((tiles, tile_rows, width), bf16),
            pltpu.VMEM((tiles, tile_rows, columns // 2), bf16),
            pltpu.VMEM((columns // 2, width), bf16),
            pltpu.SemaphoreType.DMA((len(wides) + 1,)),
            pltpu.SemaphoreType.DMA((tiles,)),
            pltpu.SemaphoreType.DMA((tiles,)),
            pltpu.SemaphoreType.DMA((max(tiles, 2 * len(blocks)),)),
        ],
        compiler_params=pltpu.CompilerParams(vmem_limit_bytes=vmem_limit),
        cost_estimate=pl.CostEstimate(
            flops=3 * rows * columns * width,
            bytes_accessed=2 * rows * (wide + 2 * width) + 3 * columns * width,
            transcendentals=rows * columns // 2,
        ),
        name="slots_block",
    )(where, *blocks, *sources, *downs, *earlier)


def after(value, *events):
    return lax.optimization_barrier((value, *events))[0]


def chip_gather(block):
    return [block] + [swap(block, "expert", bits) for bits in (2, 4, 6)]


def core_gather(chips):
    return chips + [swap(chip, "expert", 1) for chip in chips]


def stage(*values):
    return lax.optimization_barrier(values)


def add(left, right):
    return (left.astype(f32) + right.astype(f32)).astype(bf16)


def quarter_body(
    head_outputs,
    residual,
    output_weight,
    router,
    norm_gain,
    placed_gate_up,
    placed_down,
    routes,
    replica_pick,
    placement,
    final_gain,
):
    rows, width = residual.shape
    slots, depth, columns = placed_gate_up.shape
    devices, shards = lax.axis_size("expert"), lax.axis_size("shard")
    e, s = lax.axis_index("expert"), lax.axis_index("shard")
    inner = (s == 1) | (s == 2)
    where = jnp.stack([e, s, inner]).astype(jnp.int32)
    hidden_units = columns // 2
    units = hidden_units // shards

    piece = output_weight.shape[0] // devices
    own = lax.dynamic_slice_in_dim(output_weight, e * piece, piece, 0)
    over_z = jnp.stack([own] + [swap(own, "shard", k) for k in range(1, shards)])

    sends = [quarters(placed_gate_up, *chunks[0], shards)]

    def exchange(send):
        return lax.all_to_all(send, "shard", split_axis=0, concat_axis=0, tiled=True)

    over_z, send, where = stage(over_z, sends[0], where)
    weights = [exchange(send)]
    down = placed_down.reshape(slots * units, width)
    pieces = chip_gather(over_z)
    sends.append(quarters(after(placed_gate_up, pieces[1]), *chunks[1], shards))
    *pieces, other_down, sends[1] = stage(*pieces, swap(after(down, over_z), "expert", 1), sends[1])
    pieces = core_gather(pieces)
    downs = [down, other_down]
    block, hidden = project(where, head_outputs, residual, norm_gain, router, routes, replica_pick, placement, pieces)

    cross = [(1, 2), (2, 1)]
    outward = [(1, 0), (2, 3)]

    own_chips = chip_gather(block)
    near = swap(block, "shard", 1)
    first_in = lax.ppermute(block, "shard", cross)
    second_in = lax.ppermute(near, "shard", cross)
    parts = [lax.dynamic_index_in_dim(sends[1], s ^ k, 0, keepdims=False) for k in range(shards)]
    near, first_in, second_in, *rest = stage(near, first_in, second_in, *parts, *own_chips)
    parts, own_chips = rest[:4], rest[4:]

    near_chips = [near, swap(near, "expert", 2), swap(near, "expert", 4)]
    first_out = lax.ppermute(first_in, "shard", outward)
    second_out = lax.ppermute(second_in, "shard", outward)
    part_in = lax.ppermute(parts[3], "shard", cross)
    first_out, second_out, weights[0], part_in, *rest = stage(
        first_out, second_out, weights[0], part_in, *parts, *near_chips
    )
    parts, near_chips = list(rest[:4]), list(rest[4:])

    parts[1] = swap(parts[1], "shard", 1)
    parts[2] = swap(parts[2], "shard", 2)
    far = jnp.concatenate([jnp.where(inner, first_in, first_out), jnp.where(inner, second_in, second_out)])
    far_chips = chip_gather(far)

    weights = [[weights[0]]]
    others = [[swap(weights[0][0], "expert", 1)]]
    def run(blocks, which, earlier, cut=None):
        sources, sets = [], []
        for chunk in range(len(chunks))[which]:
            sources += [weights[chunk], others[chunk]]
            sets += [(0, *chunks[chunk]), (1, *chunks[chunk])]
        return slots_block(where, rows, blocks, sources, tuple(sets), downs, earlier, slots, cut)

    own_blocks = [(chip, 0) for chip in own_chips]
    (early,) = run(own_blocks, slice(0, 1), [])
    early, *rest = stage(early, *parts[1:], near_chips[0], *far_chips)
    parts[1:], near_chips[0], far_chips = rest[:3], rest[3], rest[4:]

    part_out = lax.ppermute(parts[3], "shard", [(0, 3), (3, 0)])
    near_blocks = [(chip, 0) for chip in near_chips + [swap(near_chips[0], "expert", 6)]]
    far_blocks = [(chip, first) for first in (0, rows) for chip in far_chips]
    (late,) = run(far_blocks, slice(0, 1), [])
    (middle,) = run(near_blocks, slice(0, 1), [])
    part_out, late, middle = stage(part_out, late, middle)
    parts[3:] = [part_in, part_out]
    weights.append(parts)
    others.append([swap(part, "expert", 1) for part in parts])

    sums = {}
    far = run(far_blocks, slice(1, 2), [(late, 0), (late, tile_rows)], "labelled")
    far_x, far_y = swap(far[0], "expert", 2), swap(far[1], "expert", 4)
    close = run(near_blocks + own_blocks, slice(1, 2), [(middle, 0), (after(early, far[2]), 0)], "ordered")
    far_x, far_y, *close = stage(far_x, far_y, *close)
    close_x, close_y = swap(close[0], "expert", 2), swap(close[1], "expert", 4)
    for pair, left, right, a_x, b_y in (
        ((3, 2), far[2], far[3], far_x, far_y), ((1, 0), close[2], close[3], close_x, close_y)
    ):
        a_y = swap(add(left[1], a_x[1]), "expert", 4)
        b_x = swap(add(right[1], b_y[1]), "expert", 2)
        left = left[0].astype(f32) + a_x[0].astype(f32) + a_y.astype(f32)
        right = right[0].astype(f32) + b_y[0].astype(f32) + b_x.astype(f32)
        for i, k in enumerate(pair):
            sums[k] = jnp.concatenate([left[i], right[i]], axis=1)
    sent = [swap(sums[k].astype(bf16), "shard", k) for k in range(1, shards)]
    total = hidden.astype(f32) + sums[0]
    for part in sent:
        total = total + part.astype(f32)
    return rms_scale(total, final_gain).astype(bf16)


def choose_slots(routes, replica_pick, placement, experts):
    labels = jnp.arange(experts, dtype=jnp.int32)
    holder_mask = (placement[None, :] == labels[:, None]).astype(jnp.int32)
    before = jnp.cumsum(holder_mask, axis=1) - holder_mask
    copies = jnp.sum(holder_mask, axis=1)
    places = jnp.arange(placement.shape[0], dtype=jnp.int32)
    route_hits = (routes[..., None] == labels).astype(jnp.int32)
    held_count = jnp.sum(route_hits * copies, axis=-1)
    wanted = replica_pick % held_count
    chosen = jnp.zeros(routes.shape, jnp.int32)
    for replica in range(most_copies):
        column = jnp.sum(
            holder_mask * (before == replica).astype(jnp.int32) * places[None, :], axis=1
        )
        candidate = jnp.sum(route_hits * column, axis=-1)
        chosen = jnp.where(wanted == replica, candidate, chosen)
    return chosen


def padded_experts(inbound, gate_up, down_proj):
    sources, slot_count, slot_depth, model_width = inbound.shape
    per_source = slot_count * slot_depth
    upper_bound = max(1, 1024 // per_source)
    power_two = 1 << upper_bound.bit_length() - 1
    group_size = math.gcd(sources, power_two)
    stacked = inbound.reshape(
        sources // group_size, group_size, slot_count, slot_depth, model_width
    )
    hidden_units = down_proj.shape[1]

    def apply_block(block_part):
        both_parts = jnp.einsum(
            "bjmd,jdf->bjmf", block_part, gate_up, preferred_element_type=jnp.float32
        )
        activated = (
            jax.nn.silu(both_parts[..., :hidden_units]) * both_parts[..., hidden_units:]
        ).astype(jnp.bfloat16)
        return jnp.einsum(
            "bjmf,jfd->bjmd", activated, down_proj, preferred_element_type=jnp.float32
        ).astype(jnp.bfloat16)

    return lax.map(apply_block, stacked).reshape(inbound.shape)


def body(
    head_outputs,
    residual,
    output_weight,
    router,
    norm_gain,
    placed_gate_up,
    placed_down,
    routes,
    replica_pick,
    placement,
    final_gain,
):
    row_count, model_width = residual.shape
    route_count = routes.shape[1]
    experts = router.shape[1]
    place_count = placement.shape[0]
    groups = lax.axis_size("expert")
    slot_count = place_count // groups
    capacity = CAP
    projected = jnp.dot(
        head_outputs,
        lax.all_gather(output_weight, "shard", axis=0, tiled=True),
        preferred_element_type=jnp.float32,
    )
    hidden = (residual.astype(jnp.float32) + projected).astype(jnp.bfloat16)
    hidden_wide = hidden.astype(jnp.float32)
    normed = rms_scale(hidden_wide, norm_gain).astype(jnp.bfloat16)
    logits = jnp.dot(normed, router, preferred_element_type=jnp.float32)
    labels = jnp.arange(experts, dtype=jnp.int32)
    selector = (routes[..., None] == labels).astype(jnp.float32)
    chosen_logits = jnp.sum(selector * logits[:, None, :], axis=-1)
    raised = jnp.exp(chosen_logits)
    route_weight = raised / jnp.sum(raised, axis=-1, keepdims=True)
    slot_ids = choose_slots(routes, replica_pick, placement, experts).reshape(-1)
    slot_hits = (slot_ids[:, None] == jnp.arange(place_count, dtype=jnp.int32)).astype(jnp.int32)
    slot_rank = jnp.sum((jnp.cumsum(slot_hits, axis=0) - slot_hits) * slot_hits, axis=1)
    copies_out = jnp.repeat(normed, route_count, axis=0)
    gate_up, down_proj = (
        lax.all_gather(placed_gate_up, "shard", axis=1, tiled=True),
        lax.all_gather(placed_down, "shard", axis=1, tiled=True),
    )
    buffer_index = slot_ids * capacity + slot_rank
    outbound = (
        jnp.zeros((place_count * capacity, model_width), jnp.bfloat16)
        .at[buffer_index]
        .set(copies_out)
    )
    inbound = lax.all_to_all(
        outbound.reshape(groups, slot_count * capacity, model_width),
        "expert",
        split_axis=0,
        concat_axis=0,
        tiled=True,
    )
    inbound = inbound.reshape(groups, slot_count, capacity, model_width)
    answers = padded_experts(inbound, gate_up, down_proj)
    returned = lax.all_to_all(
        answers.reshape(groups, slot_count * capacity, model_width),
        "expert",
        split_axis=0,
        concat_axis=0,
        tiled=True,
    )
    returned = returned.reshape(place_count * capacity, model_width)
    gathered = returned[buffer_index].reshape(row_count, route_count, model_width)
    mixture = jnp.sum(route_weight[..., None] * gathered.astype(jnp.float32), axis=1)
    return rms_scale(hidden_wide + mixture, final_gain).astype(jnp.bfloat16)


def solution(mesh):
    by_quarters = mesh.shape["expert"] == 8 and mesh.shape["shard"] == 4
    return jax.shard_map(
        quarter_body if by_quarters else body,
        mesh=mesh,
        in_specs=(
            P(("expert", "shard"), None),
            P(("expert", "shard"), None),
            P("shard", None),
            P(),
            P(),
            P("expert", "shard", None),
            P("expert", "shard", None),
            P(("expert", "shard"), None),
            P(("expert", "shard"), None),
            P(),
            P(),
        ),
        out_specs=P(("expert", "shard"), None),
        check_vma=False,
    )
```
